256 devices in a mesh: ctx: 64 (over x, z, core), head: 4 (over y).
Axes of the slice: x: 4, y: 4, z: 8, core: 2. Of those that a mesh axis runs over, the one named last changes fastest.
Arguments:
- queries: bfloat16 [8192, 4096], P('ctx', 'head'), may hold values from -100 to 100
- keys: bfloat16 [8192, 1024], P('ctx', 'head'), may hold values from -5 to 5
- values: bfloat16 [8192, 1024], P('ctx', 'head'), may hold values from -6 to 6
- grad_attn: bfloat16 [8192, 4096], P('ctx', 'head'), may hold values from -6 to 6
- ssm_input: bfloat16 [8192, 4096], P('ctx', 'head'), may hold values from -6 to 6
- ssm_b: bfloat16 [8192, 256], P('ctx'), may hold values from -0.375 to 0.375
- ssm_c: bfloat16 [8192, 256], P('ctx'), may hold values from -0.375 to 0.375
- log_decay: float32 [64, 8192], P('head', 'ctx'), may hold values from -1 to 0
- skip_gain: float32 [64], P('head'), may hold values from 0.5 to 1.5
- grad_ssm: bfloat16 [8192, 4096], P('ctx', 'head'), may hold values from -6 to 6
- doc_lengths: int32 [32], replicated, may hold values from 1 to 512, 8192 in all
Outputs:
- grad_queries: bfloat16 [8192, 4096], P('ctx', 'head')
- grad_keys: bfloat16 [8192, 1024], P('ctx', 'head')
- grad_values: bfloat16 [8192, 1024], P('ctx', 'head')
- grad_input: bfloat16 [8192, 4096], P('ctx', 'head')
- grad_b: bfloat16 [8192, 256], P(('ctx', 'head'))
- grad_c: bfloat16 [8192, 256], P(('ctx', 'head'))
The draws below stay inside these ranges and needn't reach their ends.
Inputs may be any that keep to these rules, and one draw needn't show every extreme that they name: `doc_lengths`: they sum to 8192, and the longest document has exactly 512 tokens.
All inputs are finite; a program needn't handle non-finite values.
Results may differ from the reference program's by a relative error of at most 0.0065.
Values may be sent and summed in bfloat16 or wider, within the bound.
A program may use at most 320 MiB of HBM per device.

```python
import math
import jax
import jax.numpy as jnp
import numpy as np
from jax import lax

D_HEAD = 128
AHEADS = 32
KVHEADS = 8
MHEADS = 64
MDIM = 64
NSTATE = 256
PREV = 4
TOK_DEV = 128
PACK_TOKENS = 8192
LONGEST_DOCUMENT = 512
DOCS = 32


def shared_attention(key):
    base_query = jnp.clip(jax.random.normal(jax.random.fold_in(key, 101), (PACK_TOKENS, AHEADS, D_HEAD), jnp.float32), -4.0, 4.0)
    base_key = jnp.clip(jax.random.normal(jax.random.fold_in(key, 102), (PACK_TOKENS, KVHEADS, D_HEAD), jnp.float32), -4.0, 4.0)
    return (base_query, base_key)


def draw_queries(key, part):
    base_query, base_key = shared_attention(key)
    result = base_query
    return result.reshape(PACK_TOKENS, AHEADS * D_HEAD).astype(jnp.bfloat16)


def draw_keys(key, part):
    base_query, base_key = shared_attention(key)
    result = base_key
    return result.reshape(PACK_TOKENS, KVHEADS * D_HEAD).astype(jnp.bfloat16)


def draw_log_decay(key, part):
    key = jax.random.fold_in(key, 5)
    sequence_pieces = jax.random.split(key, 6)
    slow_share = 0.5
    slow = jax.random.uniform(sequence_pieces[0], (MHEADS, 1), jnp.float32) < slow_share
    fast_rate = jnp.exp(jax.random.uniform(sequence_pieces[1], (MHEADS, 1), jnp.float32, jnp.log(1.0 / 50.0), jnp.log(1.0 / 30.0)))
    slow_rate = jnp.exp(jax.random.uniform(sequence_pieces[2], (MHEADS, 1), jnp.float32, jnp.log(0.3 / LONGEST_DOCUMENT), jnp.log(2.0 / LONGEST_DOCUMENT)))
    spike_probability = jnp.where(slow, slow_rate, fast_rate)
    length_noise = jnp.exp(jax.random.uniform(sequence_pieces[3], (MHEADS, PACK_TOKENS), jnp.float32, jnp.log(0.5), jnp.log(2.0)))
    spike_sample = jax.random.uniform(sequence_pieces[4], (1, PACK_TOKENS), jnp.float32)
    spike_length = jnp.log(1.0 - 0.2 - 0.3 * jax.random.uniform(sequence_pieces[5], (1, PACK_TOKENS), jnp.float32))
    length_spike = jnp.where(spike_sample < 3.0 / LONGEST_DOCUMENT, spike_length, 0.0)
    return -spike_probability * length_noise + length_spike


def level_of(stream_key, extent, shards, least, top_value):
    def one(position, parts):
        heights = jax.random.uniform(jax.random.fold_in(jax.random.fold_in(stream_key, 6), position), (parts,), jnp.float32, least / len(shards), top_value / len(shards))
        return jnp.repeat(jnp.exp(heights), extent[position] // parts).reshape((-1,) + (1,) * (len(extent) - position - 1))

    factor_of = one(*shards[0])
    for cut in shards[1:]:
        factor_of = factor_of * one(*cut)
    return factor_of


def profile(number_of, total, bound, skew):
    loads = [(1 << 20) // math.isqrt(grade ** skew) + 1 for grade in range(2, number_of + 1)]
    spare, counts = total - bound - (number_of - 1), [1] * (number_of - 1)
    while spare > 0:
        free = [i for i in range(number_of - 1) if counts[i] < bound]
        pool, remaining = sum([loads[i] for i in free]), spare
        for i in free:
            more = min(bound - counts[i], max(1, remaining * loads[i] // pool), spare)
            counts[i] = counts[i] + more
            spare = spare - more
    return np.array([bound] + counts)


def ragged_sizes(stream_key, count, total, reach, lean):
    if count == 2:
        one = jax.random.randint(stream_key, (), max(1, total - reach), min(reach, total - 1) + 1)
        return jnp.stack([one, total - one])
    sizes = jnp.asarray(profile(count, total, reach, lean), jnp.int32)
    pairs = (count - 1) // 2
    giver, sink = sizes[1:1 + 2 * pairs:2], sizes[2:2 + 2 * pairs:2]
    margin = jnp.minimum(giver - 1, reach - sink)
    passed = jax.random.randint(jax.random.fold_in(stream_key, 1), (pairs,), 0, 1 << 20) % (margin + 1)
    sizes = sizes.at[1:1 + 2 * pairs:2].set(giver - passed).at[2:2 + 2 * pairs:2].set(sink + passed)
    return sizes[jax.random.permutation(jax.random.fold_in(stream_key, 2), count)]


def noise(key, dims, width, reach, shards=(), kind=jnp.bfloat16):
    entries = width * jax.random.normal(key, dims, jnp.float32)
    if shards:
        entries = entries * level_of(key, dims, shards, -0.22, 0.18)
    return jnp.clip(entries, -reach, reach).astype(kind)


def setup_inputs(seed: int = 0) -> dict:
    arg_keys = jax.random.split(jax.random.key(seed), 12)
    return {
        "queries": draw_queries(jax.random.fold_in(arg_keys[11], 71), 0),
        "keys": draw_keys(jax.random.fold_in(arg_keys[11], 71), 0),
        "values": noise(arg_keys[2], (PACK_TOKENS, KVHEADS * D_HEAD), 1.0, 6.0, ((0, 64), (1, 4))),
        "grad_attn": noise(arg_keys[3], (PACK_TOKENS, AHEADS * D_HEAD), 1.0, 6.0, ((0, 64), (1, 4))),
        "ssm_input": noise(arg_keys[4], (PACK_TOKENS, MHEADS * MDIM), 1.0, 6.0, ((0, 64), (1, 4))),
        "ssm_b": noise(arg_keys[5], (PACK_TOKENS, NSTATE), NSTATE ** -0.5, 0.375, ((0, 64),)),
        "ssm_c": noise(arg_keys[6], (PACK_TOKENS, NSTATE), NSTATE ** -0.5, 0.375, ((0, 64),)),
        "log_decay": draw_log_decay(jax.random.fold_in(arg_keys[11], 71), 0),
        "skip_gain": jnp.clip(0.5 + 1.0 * jax.random.uniform(arg_keys[8], (MHEADS,), jnp.float32) ** level_of(arg_keys[8], (MHEADS,), ((0, 4),), -0.2, 0.2), 0.5, 1.5),
        "grad_ssm": noise(arg_keys[9], (PACK_TOKENS, MHEADS * MDIM), 1.0, 6.0, ((0, 64), (1, 4))),
        "doc_lengths": ragged_sizes(arg_keys[10], DOCS, PACK_TOKENS, LONGEST_DOCUMENT, 1).astype(jnp.int32),
    }


HIGH = lax.Precision.HIGHEST

def document_of(positions, lengths):
    ends = jnp.cumsum(lengths).astype(jnp.int32)
    return lax.optimization_barrier(jnp.sum((positions[:, None] >= ends[None, :]).astype(jnp.int32), axis=1)).astype(jnp.int32)

def attention_grads(query_in, key_in, value_in, grad_out, query_pos, key_pos, lengths, head_size):
    query_count = query_in.shape[0]
    key_count = key_in.shape[0]
    groups = key_in.shape[1] // head_size
    ratio = query_in.shape[1] // key_in.shape[1]
    score_scale = 1.0 / math.sqrt(head_size)
    query_doc = document_of(query_pos, lengths)
    key_doc = document_of(key_pos, lengths)
    allowed = (query_doc[:, None] == key_doc[None, :]) & (key_pos[None, :] <= query_pos[:, None]) & (key_pos[None, :] >= 0)
    query_grp = query_in.astype(jnp.float32).reshape(query_count, groups, ratio, head_size).transpose(1, 0, 2, 3)
    grad_grp = grad_out.astype(jnp.float32).reshape(query_count, groups, ratio, head_size).transpose(1, 0, 2, 3)
    key_grp = key_in.astype(jnp.float32).reshape(key_count, groups, head_size).transpose(1, 0, 2)
    value_grp = value_in.astype(jnp.float32).reshape(key_count, groups, head_size).transpose(1, 0, 2)

    def one_group(operands):
        query_h, key_h, value_h, grad_h = operands
        scores = jnp.einsum('qre,ke->rqk', query_h, key_h, precision=HIGH) * score_scale
        scores = jnp.where(allowed[None], scores, -1e+30)
        row_peak = lax.optimization_barrier(jnp.max(scores, axis=2, keepdims=True))
        weights = jnp.exp(scores - row_peak)
        normed = weights / lax.optimization_barrier(jnp.sum(weights, axis=2, keepdims=True))
        dprobs = jnp.einsum('qre,ke->rqk', grad_h, value_h, precision=HIGH)
        centre = lax.optimization_barrier(jnp.sum(normed * dprobs, axis=2, keepdims=True))
        dscores = normed * (dprobs - centre)
        dscores_low = dscores.astype(jnp.bfloat16).astype(jnp.float32)
        probs_low = normed.astype(jnp.bfloat16).astype(jnp.float32)
        grad_query = jnp.einsum('rqk,ke->qre', dscores_low, key_h, precision=HIGH) * score_scale
        grad_key = jnp.einsum('rqk,qre->ke', dscores_low, query_h, precision=HIGH) * score_scale
        grad_value = jnp.einsum('rqk,qre->ke', probs_low, grad_h, precision=HIGH)
        return (grad_query, grad_key, grad_value)
    grad_query, grad_key, grad_value = lax.map(one_group, (query_grp, key_grp, value_grp, grad_grp))
    grad_query = grad_query.transpose(1, 0, 2, 3).reshape(query_count, groups * ratio * head_size)
    grad_key = grad_key.transpose(1, 0, 2).reshape(key_count, groups * head_size)
    grad_value = grad_value.transpose(1, 0, 2).reshape(key_count, groups * head_size)
    return (grad_query, grad_key, grad_value)

def ssd_block(inputs_x, outgrad, b_rows, c_rows, decay_log, token_doc, doc_before):
    cumul = jnp.cumsum(decay_log, axis=1)
    length = token_doc.shape[0]
    order = jnp.arange(length, dtype=jnp.int32)
    causal = (order[:, None] >= order[None, :]) & (token_doc[:, None] == token_doc[None, :])
    differ = cumul[:, :, None] - cumul[:, None, :]
    within = jnp.where(causal[None], jnp.exp(jnp.where(causal[None], differ, 0.0)), 0.0)
    pairs = jnp.einsum('thp,shp->hts', outgrad, inputs_x, precision=HIGH)
    mixed = within * pairs
    carried_in = jnp.exp(cumul) * (token_doc == doc_before).astype(jnp.float32)[None, :]
    last_doc = token_doc[length - 1]
    to_end = jnp.exp(cumul[:, length - 1:] - cumul) * (token_doc == last_doc).astype(jnp.float32)[None, :]
    through = jnp.exp(cumul[:, length - 1]) * (last_doc == doc_before).astype(jnp.float32)
    state_local = jnp.einsum('hs,sn,shp->hnp', to_end, b_rows, inputs_x, precision=HIGH)
    adjoint_local = jnp.einsum('hs,sn,shp->hnp', carried_in, c_rows, outgrad, precision=HIGH)
    return (within, mixed, carried_in, to_end, through, state_local, adjoint_local)

def ssd_grads_c(sequence_pieces, b_rows, outgrad, state_in):
    within, mixed, carried_in, to_end, through, state_local, adjoint_local = sequence_pieces
    return jnp.einsum('hts,sn->tn', mixed, b_rows, precision=HIGH) + jnp.einsum('ht,hnp,thp->tn', carried_in, state_in, outgrad, precision=HIGH)

def ssd_grads_xb(sequence_pieces, inputs_x, outgrad, b_rows, c_rows, gains, adjoint_in):
    within, mixed, carried_in, to_end, through, state_local, adjoint_local = sequence_pieces
    couple = jnp.dot(b_rows, c_rows.T, precision=HIGH)
    back_mix = jnp.transpose(within, (0, 2, 1)) * couple[None]
    grad_x = jnp.einsum('hts,shp->thp', back_mix, outgrad, precision=HIGH) + jnp.einsum('ht,tn,hnp->thp', to_end, b_rows, adjoint_in, precision=HIGH) + gains[None, :, None] * outgrad
    grad_bb = jnp.einsum('hst,sn->tn', mixed, c_rows, precision=HIGH) + jnp.einsum('ht,hnp,thp->tn', to_end, adjoint_in, inputs_x, precision=HIGH)
    return (grad_x, grad_bb)

def reference(queries, keys, values, grad_attn, ssm_input, ssm_b, ssm_c, log_decay, skip_gain, grad_ssm, doc_lengths):
    block = TOK_DEV
    nblocks = PACK_TOKENS // block
    pad_rows = PREV * block
    window = (PREV + 1) * block
    key_pad = jnp.concatenate([jnp.zeros((pad_rows, keys.shape[1]), keys.dtype), keys], axis=0)
    value_pad = jnp.concatenate([jnp.zeros((pad_rows, values.shape[1]), values.dtype), values], axis=0)
    numbers = jnp.arange(nblocks, dtype=jnp.int32)

    def attend_step(carry, number):
        gkey_pad, gvalue_pad = carry
        start = (number * block).astype(jnp.int32)
        query_blk = lax.dynamic_slice_in_dim(queries, start, block, 0)
        grad_blk = lax.dynamic_slice_in_dim(grad_attn, start, block, 0)
        key_win = lax.dynamic_slice_in_dim(key_pad, start, window, 0)
        value_win = lax.dynamic_slice_in_dim(value_pad, start, window, 0)
        query_pos = start + jnp.arange(block, dtype=jnp.int32)
        key_pos = start - pad_rows + jnp.arange(window, dtype=jnp.int32)
        grad_query, grad_key, grad_value = attention_grads(query_blk, key_win, value_win, grad_blk, query_pos, key_pos, doc_lengths, D_HEAD)
        gkey_pad = lax.dynamic_update_slice_in_dim(gkey_pad, lax.dynamic_slice_in_dim(gkey_pad, start, window, 0) + grad_key, start, 0)
        gvalue_pad = lax.dynamic_update_slice_in_dim(gvalue_pad, lax.dynamic_slice_in_dim(gvalue_pad, start, window, 0) + grad_value, start, 0)
        return ((gkey_pad, gvalue_pad), grad_query)
    zero_pad = jnp.zeros((PACK_TOKENS + pad_rows, keys.shape[1]), jnp.float32)
    (gkey_pad, gvalue_pad), grad_query_all = lax.scan(attend_step, (zero_pad, zero_pad), numbers)
    grad_queries = grad_query_all.reshape(PACK_TOKENS, queries.shape[1]).astype(jnp.bfloat16)
    grad_keys = gkey_pad[pad_rows:].astype(jnp.bfloat16)
    grad_values = gvalue_pad[pad_rows:].astype(jnp.bfloat16)

    def block_parts(number):
        start = (number * block).astype(jnp.int32)
        inputs_x = lax.dynamic_slice_in_dim(ssm_input, start, block, 0).astype(jnp.float32).reshape(block, MHEADS, MDIM)
        outgrad = lax.dynamic_slice_in_dim(grad_ssm, start, block, 0).astype(jnp.float32).reshape(block, MHEADS, MDIM)
        b_rows = lax.dynamic_slice_in_dim(ssm_b, start, block, 0).astype(jnp.float32)
        c_rows = lax.dynamic_slice_in_dim(ssm_c, start, block, 0).astype(jnp.float32)
        decay_log = lax.dynamic_slice_in_dim(log_decay, start, block, 1)
        positions = start + jnp.arange(block, dtype=jnp.int32)
        token_doc = document_of(positions, doc_lengths)
        before = document_of(jnp.reshape(start - 1, (1,)).astype(jnp.int32), doc_lengths)[0]
        doc_before = jnp.where(start > 0, before, -1).astype(jnp.int32)
        sequence_pieces = ssd_block(inputs_x, outgrad, b_rows, c_rows, decay_log, token_doc, doc_before)
        return (sequence_pieces, inputs_x, outgrad, b_rows, c_rows)

    def forward_step(state_in, number):
        sequence_pieces, inputs_x, outgrad, b_rows, c_rows = block_parts(number)
        grad_cc = ssd_grads_c(sequence_pieces, b_rows, outgrad, state_in)
        state_out = sequence_pieces[4][:, None, None] * state_in + sequence_pieces[5]
        return (state_out, grad_cc)

    def backward_step(adjoint_in, number):
        sequence_pieces, inputs_x, outgrad, b_rows, c_rows = block_parts(number)
        grad_x, grad_bb = ssd_grads_xb(sequence_pieces, inputs_x, outgrad, b_rows, c_rows, skip_gain, adjoint_in)
        adjoint_out = sequence_pieces[4][:, None, None] * adjoint_in + sequence_pieces[6]
        return (adjoint_out, (grad_x, grad_bb))
    zero_state = jnp.zeros((MHEADS, NSTATE, MDIM), jnp.float32)
    _, grad_c_all = lax.scan(forward_step, zero_state, numbers)
    _, (grad_x_all, grad_b_all) = lax.scan(backward_step, zero_state, numbers, reverse=True)
    grad_input = grad_x_all.reshape(PACK_TOKENS, MHEADS * MDIM).astype(jnp.bfloat16)
    grad_b = grad_b_all.reshape(PACK_TOKENS, NSTATE).astype(jnp.bfloat16)
    grad_c = grad_c_all.reshape(PACK_TOKENS, NSTATE).astype(jnp.bfloat16)
    return (grad_queries, grad_keys, grad_values, grad_input, grad_b, grad_c)
```

```python
import math

import jax
import jax.numpy as jnp
from jax import lax
from jax.experimental import pallas as pl
from jax.experimental.pallas import tpu as pltpu
from jax.sharding import PartitionSpec as P

D_HEAD = 128
MDIM = 64
REACH = 4
SLOTS = REACH + 2

F32 = jnp.float32
BF16 = jnp.bfloat16
MESH = pl.DeviceIdType.MESH
HIGH = lax.Precision.HIGHEST


def dot(a, b, over, precision=None):
    return lax.dot_general(
        a, b, ((over[:1], over[1:]), ((), ())), precision=precision, preferred_element_type=F32
    )


def iota(shape, dim):
    return lax.broadcasted_iota(jnp.int32, shape, dim)


def document_starts(lens, base, tok):
    docs = lens.shape[1]
    row, col = iota((docs, docs), 0), iota((docs, docs), 1)
    lens_row = jnp.broadcast_to(lens.astype(F32), (docs, docs))
    lens_col = jnp.sum(jnp.where(row == col, lens_row, 0.0), axis=1, keepdims=True)
    ends_col = jnp.sum(jnp.where(col <= row, lens_row, 0.0), axis=1, keepdims=True)
    ends_row = jnp.sum(jnp.where(row <= col, lens_col, 0.0), axis=0, keepdims=True)
    at_col = (base + iota((tok, docs), 0)).astype(F32)
    at_row = (base + iota((docs, tok), 1)).astype(F32)
    start_col = jnp.max(jnp.where(at_col >= ends_row, ends_row, 0.0), axis=1, keepdims=True)
    start_row = jnp.max(jnp.where(at_row >= ends_col, ends_col, 0.0), axis=0, keepdims=True)
    return start_col, start_row


def kernel(
    shards,
    ways,
    q_ref,
    k_ref,
    v_ref,
    do_ref,
    x_ref,
    b_ref,
    c_ref,
    decay_ref,
    skip_ref,
    g_ref,
    lens_ref,
    dq_ref,
    dk_ref,
    dv_ref,
    dx_ref,
    db_ref,
    dc_ref,
    kv,
    fx,
    bg,
    fth,
    bth,
    dkv,
    mate_out,
    mate_in,
    far_out,
    far_in,
    near_out,
    near_in,
    probs,
    dscores,
    to_end,
    dx_acc,
    grads,
    y_out,
    y_in,
    send,
    recv,
):
    tok, heads = q_ref.shape[0], decay_ref.shape[0]
    kw = k_ref.shape[1]
    groups = kw // D_HEAD
    ratio = q_ref.shape[1] // kw
    width = x_ref.shape[1]
    state = b_ref.shape[1]
    shard = lax.axis_index("ctx")
    way = lax.axis_index("head")
    core = lax.rem(shard, 2)
    mate = (shard + 1 - 2 * core, way)
    up = (lax.rem(shard + 2, shards), way)
    down = (lax.rem(shard + shards - 2, shards), way)
    others = [(shard, lax.rem(way + j, ways)) for j in range(1, ways)]

    barrier = pltpu.get_barrier_semaphore()
    for peer in [mate, up, down] + others:
        pl.semaphore_signal(barrier, inc=1, device_id=peer, device_id_type=MESH)

    def rows(slot, size=tok):
        return pl.ds(pl.multiple_of(slot * size, size), size)

    def copy(ref, source, target, peer, number):
        return pltpu.make_async_remote_copy(
            src_ref=ref if source is None else ref.at[source],
            dst_ref=target,
            send_sem=send.at[number],
            recv_sem=recv.at[number],
            device_id=peer,
            device_id_type=MESH,
        )

    started = []

    def put(ref, source, target, peer, number):
        one = copy(ref, source, target, peer, number)
        one.start()
        started.append(one)

    def arrived(ref, source, number):
        copy(ref, source, ref.at[source], mate, number).wait_recv()

    class Halo:
        def __init__(self, ref, size, upward, first):
            self.ref, self.size, self.first = ref, size, first
            self.own, self.near, self.far = (4, 2, 0) if upward else (0, 2, 4)
            self.peer = up if upward else down

        def at(self, slot):
            return rows(slot, self.size)

        def send(self, slot, peer, number, target=None):
            place = self.at(slot if target is None else target)
            put(self.ref, self.at(slot), self.ref.at[place], peer, self.first + number)

        def begin(self):
            self.send(self.own + core, self.peer, 1, self.near + core)

        def begin_mate(self):
            self.send(self.own + core, mate, 0)

        def relay(self):
            arrived(self.ref, self.at(self.near + core), self.first + 1)
            self.send(self.near + core, self.peer, 3, self.far + core)
            self.send(self.near + core, mate, 2)

        def finish(self):
            arrived(self.ref, self.at(self.far + core), self.first + 3)
            self.send(self.far + core, mate, 4)

        def wait(self):
            for number, slot in ((0, self.own), (2, self.near), (4, self.far)):
                arrived(self.ref, self.at(slot + 1 - core), self.first + number)

    kv_halo = Halo(kv, tok, True, 0)
    x_halo = Halo(fx, tok, True, 5)
    g_halo = Halo(bg, tok, False, 10)
    fth_halo = Halo(fth, 8, True, 15)
    bth_halo = Halo(bth, 8, False, 20)

    own = rows(4 + core)
    kv[own, 0:kw] = k_ref[...]
    kv[own, kw : 2 * kw] = v_ref[...]
    base = shard * tok
    start_col, start_row = document_starts(lens_ref[...], base, tok)
    decay = decay_ref[...]
    later = (iota((tok, tok), 0) >= iota((tok, tok), 1)).astype(F32)
    cum_col = dot(later, decay, (1, 1), HIGH)
    cum_row = dot(decay, later, (1, 1), HIGH)
    total = cum_col[tok - 1 : tok, :]
    base_f = base.astype(F32)
    last_start = start_col[tok - 1 : tok, :]
    ending = jnp.exp(total - cum_col) * (start_col == last_start).astype(F32)
    carried = jnp.exp(cum_col) * (start_col < base_f).astype(F32)
    through = jnp.exp(total) * (last_start < base_f).astype(F32)
    table = jnp.concatenate(
        [ending, carried, jnp.broadcast_to(through, (8, heads)), jnp.broadcast_to(skip_ref[...], (8, heads))],
        axis=0,
    )
    spread = (iota((heads, width), 1) // MDIM == iota((heads, width), 0)).astype(BF16)
    table_hi = table.astype(BF16)
    table_mid = (table - table_hi.astype(F32)).astype(BF16)
    table_lo = (table - table_hi.astype(F32) - table_mid.astype(F32)).astype(BF16)
    wide = dot(table_hi, spread, (1, 0)) + dot(table_mid, spread, (1, 0)) + dot(table_lo, spread, (1, 0))
    to_end[...] = wide[0:tok]
    fx[own, 0:width] = (x_ref[...].astype(F32) * wide[0:tok]).astype(BF16)
    fx[own, width : width + state] = b_ref[...]
    g_own = rows(core)
    bg[g_own, 0:width] = (g_ref[...].astype(F32) * wide[tok : 2 * tok]).astype(BF16)
    bg[g_own, width : width + state] = c_ref[...]
    th = jnp.concatenate(
        [wide[2 * tok : 2 * tok + 1, i * (width // 8) : (i + 1) * (width // 8)] for i in range(8)], axis=0
    )
    fth[rows(4 + core, 8)] = th
    bth[rows(core, 8)] = th
    skip = wide[2 * tok + 8 : 2 * tok + 9]

    pl.semaphore_wait(barrier, 3 + len(others))
    kv_halo.begin()
    g_halo.begin()
    fth_halo.begin()
    bth_halo.begin()
    kv_halo.begin_mate()
    fth_halo.begin_mate()
    bth_halo.begin_mate()
    g_halo.begin_mate()
    x_halo.begin_mate()

    causal = (iota((tok, tok), 0) >= iota((tok, tok), 1)) & (
        start_col <= (base + iota((tok, tok), 1)).astype(F32)
    )
    couple = dot(c_ref[...], b_ref[...], (1, 1))
    low = iota((tok, 2 * MDIM), 1) < MDIM

    def pair_of_heads(pair, mix):
        part = slice(pair * 2 * MDIM, (pair + 1) * 2 * MDIM)
        grad = g_ref[:, part]
        none = jnp.zeros_like(grad)
        both = jnp.concatenate([jnp.where(low, grad, none), jnp.where(low, none, grad)], axis=0)
        pairs = dot(both, x_ref[:, part], (1, 1))
        within = [
            jnp.exp(jnp.where(causal, cum_col[:, h : h + 1] - cum_row[h : h + 1, :], -1e30))
            for h in (2 * pair, 2 * pair + 1)
        ]
        back = jnp.concatenate([w * couple for w in within], axis=0).astype(BF16)
        dx_acc[:, part] = dot(back, both, (0, 0))
        return mix + pairs[0:tok] * within[0] + pairs[tok : 2 * tok] * within[1]

    mix = jnp.zeros((tok, tok), F32)
    for pair in range(heads // 4):
        mix = pair_of_heads(pair, mix)
    kv_halo.relay()
    x_halo.begin()
    for pair in range(heads // 4, heads // 2):
        mix = pair_of_heads(pair, mix)
    mix = mix.astype(BF16)
    grad_c = dot(mix, b_ref[...], (1, 0))
    grad_b = dot(mix, c_ref[...], (0, 0))
    fth_halo.relay()
    bth_halo.relay()
    kv_halo.finish()
    g_halo.relay()
    fth_halo.finish()
    bth_halo.finish()

    kv_halo.wait()
    window = (REACH + 1) * tok
    seen = pl.ds(pl.multiple_of(core * tok, tok), window)
    key_at = (base - REACH * tok + iota((window, tok), 0)).astype(F32)
    query_at = (base + iota((window, tok), 1)).astype(F32)
    allowed = (key_at <= query_at) & (key_at >= start_row)
    bias = jnp.where(allowed, 0.0, -1e30)
    bias = jnp.concatenate([bias, bias], axis=1)
    scale = 1.0 / math.sqrt(D_HEAD)
    idle = rows(5 * (1 - core))
    dkv[idle, :] = jnp.zeros((tok, 2 * kw), F32)

    def attend(group):
        keys = kv[seen, group * D_HEAD : (group + 1) * D_HEAD]
        values = kv[seen, kw + group * D_HEAD : kw + (group + 1) * D_HEAD]
        heads_of = [slice((group * ratio + r) * D_HEAD, (group * ratio + r + 1) * D_HEAD) for r in range(ratio)]
        queries = jnp.concatenate([q_ref[:, part] for part in heads_of], axis=0)
        outgrad = jnp.concatenate([do_ref[:, part] for part in heads_of], axis=0)
        for half in range(ratio // 2):
            part = slice(half * 2 * tok, (half + 1) * 2 * tok)
            scores = dot(keys, queries[part], (1, 1)) * scale + bias
            weights = jnp.exp(scores - jnp.max(scores, axis=0, keepdims=True))
            normed = weights * (1.0 / jnp.sum(weights, axis=0, keepdims=True))
            dprobs = dot(values, outgrad[part], (1, 1))
            centre = jnp.sum(normed * dprobs, axis=0, keepdims=True)
            probs[:, part] = normed.astype(BF16)
            dscores[:, part] = (normed * (dprobs - centre)).astype(BF16)
        dkv[seen, group * D_HEAD : (group + 1) * D_HEAD] = dot(dscores[...], queries, (1, 0)) * scale
        dkv[seen, kw + group * D_HEAD : kw + (group + 1) * D_HEAD] = dot(probs[...], outgrad, (1, 0))
        grad_query = dot(dscores[...], keys, (0, 0)) * scale
        for r, part in enumerate(heads_of):
            dq_ref[:, part] = grad_query[r * tok : (r + 1) * tok].astype(BF16)

    for group in range(groups):
        attend(group)
        if group == 0:
            x_halo.relay()

    for i in range(3):
        mate_out[rows(i)] = dkv[rows(2 * i + 1 - core)].astype(BF16)
    put(mate_out, None, mate_in, mate, 25)
    g_halo.finish()
    copy(mate_out, None, mate_in, mate, 25).wait_recv()
    far_out[...] = (dkv[rows(core)] + mate_in[rows(0)].astype(F32)).astype(BF16)
    put(far_out, None, far_in, down, 26)

    def carried_state(ref, ths, step):
        first = 4 + core if step < 0 else core
        value = None
        for k in range(REACH, 0, -1):
            place = first + step * k
            block = dot(ref[rows(place), width : width + state], ref[rows(place), 0:width], (0, 0))
            if value is None:
                value = block
            else:
                th = ths[rows(place, 8)]
                th = jnp.concatenate([th[i : i + 1] for i in range(8)], axis=1)
                value = block + th * value
        return value.astype(BF16)

    g_halo.wait()
    bth_halo.wait()
    fth_halo.wait()
    adjoint = carried_state(bg, bth, 1)
    grad_b = grad_b + dot(fx[own, 0:width], adjoint, (1, 1))
    dx = dx_acc[...] + dot(b_ref[...], adjoint, (1, 0)) * to_end[...] + skip * g_ref[...].astype(F32)
    dx_ref[...] = dx.astype(BF16)

    copy(far_out, None, far_in, down, 26).wait_recv()
    near = dkv[rows(2 + core)] + mate_in[rows(1)].astype(F32) + far_in[...].astype(F32)
    near_out[...] = near.astype(BF16)
    put(near_out, None, near_in, down, 27)

    x_halo.finish()
    x_halo.wait()
    grad_c = grad_c + dot(bg[g_own, 0:width], carried_state(fx, fth, -1), (1, 1))

    share = tok // ways
    grads[0:tok] = grad_b
    grads[tok : 2 * tok] = grad_c
    for j in range(ways):
        y_out[j, 0:share] = grad_b[j * share : (j + 1) * share].astype(BF16)
        y_out[j, share : 2 * share] = grad_c[j * share : (j + 1) * share].astype(BF16)
    for j, peer in enumerate(others):
        put(y_out, peer[1], y_in.at[j], peer, 28 + j)

    copy(near_out, None, near_in, down, 27).wait_recv()
    total_kv = dkv[rows(4 + core)] + mate_in[rows(2)].astype(F32) + near_in[...].astype(F32)
    dk_ref[...] = total_kv[:, 0:kw].astype(BF16)
    dv_ref[...] = total_kv[:, kw : 2 * kw].astype(BF16)

    mine = pl.multiple_of(way * share, share)
    sum_b = grads[pl.ds(mine, share)]
    sum_c = grads[pl.ds(tok + mine, share)]
    for j in range(ways - 1):
        arrived(y_in, j, 28 + j)
        sum_b = sum_b + y_in[j, 0:share].astype(F32)
        sum_c = sum_c + y_in[j, share : 2 * share].astype(F32)
    db_ref[...] = sum_b.astype(BF16)
    dc_ref[...] = sum_c.astype(BF16)
    for one in started:
        one.wait_send()


def solution(mesh):
    shards, ways = mesh.shape["ctx"], mesh.shape["head"]

    def on_device(queries, keys, values, grad_attn, ssm_input, ssm_b, ssm_c, log_decay, skip_gain, grad_ssm, doc_lengths):
        tok, kw = keys.shape
        width, state = ssm_input.shape[1], ssm_b.shape[1]
        ratio = queries.shape[1] // kw
        transfers = 28 + ways - 1
        share = tok // ways
        vmem = pl.BlockSpec(memory_space=pltpu.VMEM)
        like = lambda a: jax.ShapeDtypeStruct(a.shape, BF16)
        part = jax.ShapeDtypeStruct((share, state), BF16)
        return pl.pallas_call(
            lambda *refs: kernel(shards, ways, *refs),
            out_shape=(like(queries), like(keys), like(values), like(ssm_input), part, part),
            in_specs=[vmem] * 11,
            out_specs=(vmem,) * 6,
            scratch_shapes=[
                pltpu.VMEM((SLOTS * tok, 2 * kw), BF16),
                pltpu.VMEM((SLOTS * tok, width + state), BF16),
                pltpu.VMEM((SLOTS * tok, width + state), BF16),
                pltpu.VMEM((SLOTS * 8, width // 8), F32),
                pltpu.VMEM((SLOTS * 8, width // 8), F32),
                pltpu.VMEM((SLOTS * tok, 2 * kw), F32),
                pltpu.VMEM((3 * tok, 2 * kw), BF16),
                pltpu.VMEM((3 * tok, 2 * kw), BF16),
                pltpu.VMEM((tok, 2 * kw), BF16),
                pltpu.VMEM((tok, 2 * kw), BF16),
                pltpu.VMEM((tok, 2 * kw), BF16),
                pltpu.VMEM((tok, 2 * kw), BF16),
                pltpu.VMEM(((REACH + 1) * tok, ratio * tok), BF16),
                pltpu.VMEM(((REACH + 1) * tok, ratio * tok), BF16),
                pltpu.VMEM((tok, width), F32),
                pltpu.VMEM((tok, width), F32),
                pltpu.VMEM((2 * tok, state), F32),
                pltpu.VMEM((ways, 2 * share, state), BF16),
                pltpu.VMEM((ways - 1, 2 * share, state), BF16),
                pltpu.SemaphoreType.DMA((transfers,)),
                pltpu.SemaphoreType.DMA((transfers,)),
            ],
            compiler_params=pltpu.CompilerParams(
                collective_id=0, has_side_effects=True, vmem_limit_bytes=48 * 1024 * 1024
            ),
        )(
            queries,
            keys,
            values,
            grad_attn,
            ssm_input,
            ssm_b,
            ssm_c,
            log_decay,
            skip_gain.reshape(1, -1),
            grad_ssm,
            doc_lengths.reshape(1, -1),
        )

    both = P("ctx", "head")
    rows = P(("ctx", "head"), None)
    return jax.shard_map(
        on_device,
        mesh=mesh,
        in_specs=(both, both, both, both, both, P("ctx", None), P("ctx", None), P("head", "ctx"), P("head"), both, P()),
        out_specs=(both, both, both, both, rows, rows),
        check_vma=False,
    )
```

```python
import math

import jax
import jax.numpy as jnp
from jax import lax
from jax.experimental import pallas as pl
from jax.experimental.pallas import tpu as pltpu
from jax.sharding import PartitionSpec as P

D_HEAD = 128
MDIM = 64
REACH = 4
SLOTS = REACH + 2
TRANSFERS = 72
VMEM_BYTES = 56 * 1024 * 1024

F32 = jnp.float32
BF16 = jnp.bfloat16
MESH = pl.DeviceIdType.MESH
HIGH = lax.Precision.HIGHEST


def dot(a, b, over, precision=None):
    return lax.dot_general(
        a, b, ((over[:1], over[1:]), ((), ())), precision=precision, preferred_element_type=F32
    )


def iota(shape, dim):
    return lax.broadcasted_iota(jnp.int32, shape, dim)


def document_starts(lens, base, tok):
    docs = lens.shape[1]
    row, col = iota((docs, docs), 0), iota((docs, docs), 1)
    lens_row = jnp.broadcast_to(lens.astype(F32), (docs, docs))
    lens_col = jnp.sum(jnp.where(row == col, lens_row, 0.0), axis=1, keepdims=True)
    ends_col = jnp.sum(jnp.where(col <= row, lens_row, 0.0), axis=1, keepdims=True)
    ends_row = jnp.sum(jnp.where(row <= col, lens_col, 0.0), axis=0, keepdims=True)
    at_col = (base + iota((tok, docs), 0)).astype(F32)
    at_row = (base + iota((docs, tok), 1)).astype(F32)
    start_col = jnp.max(jnp.where(at_col >= ends_row, ends_row, 0.0), axis=1, keepdims=True)
    start_row = jnp.max(jnp.where(at_row >= ends_col, ends_col, 0.0), axis=0, keepdims=True)
    return start_col, start_row


def kernel(
    shards,
    ways,
    q_hbm,
    k_hbm,
    v_hbm,
    do_hbm,
    x_hbm,
    b_hbm,
    c_hbm,
    decay_hbm,
    skip_hbm,
    g_hbm,
    lens_hbm,
    dq_ref,
    dk_ref,
    dv_ref,
    dx_ref,
    db_ref,
    dc_ref,
    q_ref,
    do_ref,
    x_ref,
    b_ref,
    decay_ref,
    skip_ref,
    g_ref,
    lens_ref,
    kv,
    fx,
    fth,
    ga,
    gb,
    bc,
    bth,
    xs,
    dkv,
    mate_out,
    mate_in,
    far_out,
    far_in,
    near_out,
    near_in,
    probs,
    dscores,
    to_end,
    dx_acc,
    near_adjoint,
    early,
    early_out,
    early_in,
    late,
    late_out,
    late_in,
    last,
    last_out,
    last_in,
    ahead_out,
    ahead_in,
    send,
    recv,
    load,
    ready,
):
    tok, heads = q_ref.shape[0], decay_ref.shape[0]
    kw = k_hbm.shape[1]
    groups = kw // D_HEAD
    ratio = q_ref.shape[1] // kw
    width = x_ref.shape[1]
    share = tok // ways
    half = width // 2
    shard = lax.axis_index("ctx")
    way = lax.axis_index("head")
    core = lax.rem(shard, 2)

    def along(steps):
        return (lax.rem(shard + (steps + shards), shards), way)

    mate = (shard + 1 - 2 * core, way)
    up, down = along(2), along(-2)
    others = [(shard, lax.rem(way + j, ways)) for j in range(1, ways)]
    barrier = pltpu.get_barrier_semaphore()
    for peer in [along(-k) for k in range(1, REACH + 1)] + [mate] + others:
        pl.semaphore_signal(barrier, inc=1, device_id=peer, device_id_type=MESH)

    def rows(slot, size=tok):
        return pl.ds(pl.multiple_of(slot * size, size), size)

    numbers = {}

    def copy(source, target, peer, name):
        number = numbers.setdefault(name, len(numbers))
        return pltpu.make_async_remote_copy(
            src_ref=source,
            dst_ref=target,
            send_sem=send.at[number],
            recv_sem=recv.at[number],
            device_id=peer,
            device_id_type=MESH,
        )

    started = []

    def put(source, target, peer, name):
        one = copy(source, target, peer, name)
        one.start()
        started.append(one)

    def arrived(target, name):
        copy(target, target, mate, name).wait_recv()

    class Halo:
        def __init__(self, name, upward, view):
            self.name, self.view = name, view
            self.own, self.near, self.far = (4, 2, 0) if upward else (0, 2, 4)
            self.peer = up if upward else down

        def send(self, slot, peer, what, target=None):
            place = self.view(slot if target is None else target)
            put(self.view(slot), place, peer, (self.name, what))

        def begin(self):
            self.send(self.own + core, self.peer, "near", self.near + core)

        def begin_mate(self):
            self.send(self.own + core, mate, "mate own")

        def relay(self):
            arrived(self.view(self.near + core), (self.name, "near"))
            self.send(self.near + core, self.peer, "far", self.far + core)
            self.send(self.near + core, mate, "mate near")

        def finish(self):
            arrived(self.view(self.far + core), (self.name, "far"))
            self.send(self.far + core, mate, "mate far")

        def wait_near(self):
            arrived(self.view(self.own + 1 - core), (self.name, "mate own"))
            arrived(self.view(self.near + 1 - core), (self.name, "mate near"))

        def wait_far(self):
            arrived(self.view(self.far + 1 - core), (self.name, "mate far"))

    kv_halos = [Halo(("kv", i), True, lambda slot, i=i: kv.at[i, rows(slot)]) for i in range(groups)]
    x_halo = Halo("x", True, lambda slot: fx.at[rows(slot)])
    fth_halo = Halo("fth", True, lambda slot: fth.at[rows(slot, 8)])
    ga_halo = Halo("ga", False, lambda slot: ga.at[rows(slot)])
    gb_halo = Halo("gb", False, lambda slot: gb.at[rows(slot)])
    bth_halo = Halo("bth", False, lambda slot: bth.at[rows(slot, 8)])

    def c_part(slot, of):
        return bc.at[pl.ds(pl.multiple_of(slot * tok + of * share, share), share)]

    def c_spread(slot, name):
        for j, peer in enumerate(others):
            put(c_part(slot, way), c_part(slot, way), peer, ("c", name, j))

    def c_gather(slot, name):
        for j in range(ways - 1):
            arrived(c_part(slot, lax.rem(way + (ways - 1 - j), ways)), ("c", name, j))
        put(bc.at[rows(slot)], bc.at[rows(slot)], mate, ("c", "mate", name))

    own = rows(4 + core)
    g_own = rows(core)
    loads = {}
    places = [
        ("lens", lens_hbm, lens_ref),
        ("decay", decay_hbm, decay_ref),
        ("skip", skip_hbm, skip_ref),
    ]
    for i in range(groups):
        part_of = slice(i * D_HEAD, (i + 1) * D_HEAD)
        places.append(("k", k_hbm.at[:, part_of], kv.at[i, own, 0:D_HEAD]))
        places.append(("v", v_hbm.at[:, part_of], kv.at[i, own, D_HEAD : 2 * D_HEAD]))
    places += [
        ("c", c_hbm, bc.at[g_own]),
        ("g", g_hbm, g_ref),
        ("x", x_hbm, x_ref),
        ("b", b_hbm, b_ref),
        ("q", q_hbm, q_ref),
        ("do", do_hbm, do_ref),
    ]
    for number, (name, source, target) in enumerate(places):
        one = pltpu.make_async_copy(source, target, load.at[number])
        one.start()
        loads.setdefault(name, []).append(one)

    def loaded(*names):
        for name in names:
            for one in loads[name]:
                one.wait()

    loaded("lens", "decay", "skip")
    base = shard * tok
    start_col, start_row = document_starts(lens_ref[...], base, tok)
    decay = decay_ref[...]
    later = (iota((tok, tok), 0) >= iota((tok, tok), 1)).astype(F32)
    cum_col = dot(later, decay, (1, 1), HIGH)
    cum_row = dot(decay, later, (1, 1), HIGH)
    total = cum_col[tok - 1 : tok, :]
    base_f = base.astype(F32)
    last_start = start_col[tok - 1 : tok, :]
    ending = jnp.exp(total - cum_col) * (start_col == last_start).astype(F32)
    carried = jnp.exp(cum_col) * (start_col < base_f).astype(F32)
    through = jnp.exp(total) * (last_start < base_f).astype(F32)
    table = jnp.concatenate(
        [ending, carried, jnp.broadcast_to(through, (8, heads)), jnp.broadcast_to(skip_ref[...], (8, heads))],
        axis=0,
    )
    spread = (iota((heads, width), 1) // MDIM == iota((heads, width), 0)).astype(BF16)
    table_hi = table.astype(BF16)
    table_mid = (table - table_hi.astype(F32)).astype(BF16)
    table_lo = (table - table_hi.astype(F32) - table_mid.astype(F32)).astype(BF16)
    wide = dot(table_hi, spread, (1, 0)) + dot(table_mid, spread, (1, 0)) + dot(table_lo, spread, (1, 0))
    skip = wide[2 * tok + 8 : 2 * tok + 9]
    th = jnp.concatenate(
        [wide[2 * tok : 2 * tok + 1, i * (width // 8) : (i + 1) * (width // 8)] for i in range(8)], axis=0
    )
    bth[rows(core, 8)] = th
    fth[rows(4 + core, 8)] = th
    to_end[...] = wide[0:tok]

    loaded("k", "v")
    pl.semaphore_wait(barrier, REACH + 1 + len(others))
    pl.semaphore_signal(ready, inc=1, device_id=up, device_id_type=MESH)
    for halo in kv_halos:
        halo.begin()
    for halo in kv_halos:
        halo.begin_mate()
    loaded("g", "c")
    scaled = (g_ref[...].astype(F32) * wide[tok : 2 * tok]).astype(BF16)
    ga[g_own] = scaled[:, 0:half]
    gb[g_own] = scaled[:, half:]
    pl.semaphore_wait(ready, 1)
    put(c_part(core, way), c_part(2 + core, way), down, ("c", "near"))
    bth_halo.begin()
    ga_halo.begin()
    gb_halo.begin()
    loaded("x", "b")
    xs[...] = (x_ref[...].astype(F32) * wide[0:tok]).astype(BF16)
    fx[own, 0:half] = xs[:, half:]
    fx[own, half:] = b_ref[...]
    fth_halo.begin()
    for halo in (fth_halo, bth_halo, ga_halo, gb_halo, x_halo):
        halo.begin_mate()
    put(bc.at[g_own], bc.at[g_own], mate, ("c", "mate", "own"))
    state = dot(b_ref[...], xs[:, 0:half], (0, 0))

    causal = (iota((tok, tok), 0) >= iota((tok, tok), 1)) & (
        start_col <= (base + iota((tok, tok), 1)).astype(F32)
    )
    couple = dot(bc[g_own], b_ref[...], (1, 1))
    low = iota((tok, 2 * MDIM), 1) < MDIM

    def pair_of_heads(pair, mix):
        part = slice(pair * 2 * MDIM, (pair + 1) * 2 * MDIM)
        grad = g_ref[:, part]
        none = jnp.zeros_like(grad)
        both = jnp.concatenate([jnp.where(low, grad, none), jnp.where(low, none, grad)], axis=0)
        pairs = dot(both, x_ref[:, part], (1, 1))
        within = [
            jnp.exp(jnp.where(causal, cum_col[:, h : h + 1] - cum_row[h : h + 1, :], -1e30))
            for h in (2 * pair, 2 * pair + 1)
        ]
        back = jnp.concatenate([w * couple for w in within], axis=0).astype(BF16)
        dx_acc[:, part] = dot(back, both, (0, 0))
        return mix + pairs[0:tok] * within[0] + pairs[tok : 2 * tok] * within[1]

    mix = jnp.zeros((tok, tok), F32)
    for pair in range(heads // 4):
        mix = pair_of_heads(pair, mix)
    kv_halos[0].relay()
    for pair in range(heads // 4, heads // 2 - 2):
        mix = pair_of_heads(pair, mix)
    for halo in kv_halos[1:]:
        halo.relay()
    x_halo.begin()
    for pair in range(heads // 2 - 2, heads // 2):
        mix = pair_of_heads(pair, mix)
    mix = mix.astype(BF16)
    last[0:tok] = dot(mix, bc[g_own], (0, 0))
    last[tok : 2 * tok] = dot(mix, b_ref[...], (1, 0))
    arrived(c_part(2 + core, way), ("c", "near"))
    put(c_part(2 + core, way), c_part(4 + core, way), down, ("c", "far"))
    c_spread(2 + core, "near")
    bth_halo.relay()
    fth_halo.relay()
    kv_halos[0].finish()
    ga_halo.relay()
    kv_halos[1].finish()

    loaded("q", "do")
    window = (REACH + 1) * tok
    seen = pl.ds(pl.multiple_of(core * tok, tok), window)
    key_at = (base - REACH * tok + iota((window, tok), 0)).astype(F32)
    query_at = (base + iota((window, tok), 1)).astype(F32)
    allowed = (key_at <= query_at) & (key_at >= start_row)
    bias = jnp.where(allowed, 0.0, -1e30)
    bias = jnp.concatenate([bias, bias], axis=1)
    scale = 1.0 / math.sqrt(D_HEAD)
    idle = rows(5 * (1 - core))

    def attend(group):
        keys = kv[group, seen, 0:D_HEAD]
        values = kv[group, seen, D_HEAD : 2 * D_HEAD]
        heads_of = [slice((group * ratio + r) * D_HEAD, (group * ratio + r + 1) * D_HEAD) for r in range(ratio)]
        queries = jnp.concatenate([q_ref[:, part] for part in heads_of], axis=0)
        outgrad = jnp.concatenate([do_ref[:, part] for part in heads_of], axis=0)
        for half in range(ratio // 2):
            part = slice(half * 2 * tok, (half + 1) * 2 * tok)
            scores = dot(keys, queries[part], (1, 1)) * scale + bias
            weights = jnp.exp(scores - jnp.max(scores, axis=0, keepdims=True))
            normed = weights * (1.0 / jnp.sum(weights, axis=0, keepdims=True))
            dprobs = dot(values, outgrad[part], (1, 1))
            centre = jnp.sum(normed * dprobs, axis=0, keepdims=True)
            probs[:, part] = normed.astype(BF16)
            dscores[:, part] = (normed * (dprobs - centre)).astype(BF16)
        dkv[group, idle] = jnp.zeros((tok, 2 * D_HEAD), F32)
        dkv[group, seen, 0:D_HEAD] = dot(dscores[...], queries, (1, 0)) * scale
        dkv[group, seen, D_HEAD : 2 * D_HEAD] = dot(probs[...], outgrad, (1, 0))
        for i in range(3):
            mate_out[group, rows(i)] = dkv[group, rows(2 * i + 1 - core)].astype(BF16)
        put(mate_out.at[group], mate_in.at[group], mate, ("dkv mate", group))
        grad_query = dot(dscores[...], keys, (0, 0)) * scale
        for r, part in enumerate(heads_of):
            dq_ref[:, part] = grad_query[r * tok : (r + 1) * tok].astype(BF16)

    def send_far(group):
        arrived(mate_in.at[group], ("dkv mate", group))
        far_out[group] = (dkv[group, rows(core)] + mate_in[group, rows(0)].astype(F32)).astype(BF16)
        put(far_out.at[group], far_in.at[group], down, ("dkv far", group))

    def send_near(group):
        arrived(far_in.at[group], ("dkv far", group))
        near = dkv[group, rows(2 + core)] + mate_in[group, rows(1)].astype(F32) + far_in[group].astype(F32)
        near_out[group] = near.astype(BF16)
        put(near_out.at[group], near_in.at[group], down, ("dkv near", group))

    def finish_keys(group):
        arrived(near_in.at[group], ("dkv near", group))
        total_kv = dkv[group, rows(4 + core)] + mate_in[group, rows(2)].astype(F32) + near_in[group].astype(F32)
        part = slice(group * D_HEAD, (group + 1) * D_HEAD)
        dk_ref[:, part] = total_kv[:, 0:D_HEAD].astype(BF16)
        dv_ref[:, part] = total_kv[:, D_HEAD : 2 * D_HEAD].astype(BF16)

    for group in range(groups):
        kv_halos[group].wait_near()
        kv_halos[group].wait_far()
        attend(group)
        if group == 0:
            gb_halo.relay()
            x_halo.relay()
            arrived(c_part(4 + core, way), ("c", "far"))
            c_spread(4 + core, "far")
            c_gather(2 + core, "near")
        else:
            send_far(group - 1)

    def decay_through(ths, slot):
        row = ths[rows(slot, 8)]
        return jnp.concatenate([row[i : i + 1] for i in range(8)], axis=1)

    def adjoint_of(ref, k):
        return dot(bc[rows(core + k)], ref[rows(core + k)], (0, 0))

    def ahead(k, factor):
        value = state if factor is None else state * factor[:, 0:half]
        return dot(ga[rows(core + k)], value.astype(BF16), (1, 1))

    def finish_input(part, adjoint):
        last[0:tok] = last[0:tok] + dot(xs[:, part], adjoint, (1, 1))
        dx = dx_acc[:, part] + dot(b_ref[...], adjoint, (1, 0)) * to_end[:, part]
        dx_ref[:, part] = (dx + skip[:, part] * g_ref[:, part].astype(F32)).astype(BF16)

    def sum_start(held, out, into, name, first, last):
        span = pl.ds(first * share, (last - first) * share)
        for j in range(ways):
            for i in range(first, last):
                part = held[i * tok + j * share : i * tok + (j + 1) * share]
                out[j, i * share : (i + 1) * share] = part.astype(BF16)
        for j, peer in enumerate(others):
            put(out.at[peer[1], span], into.at[j, span], peer, (name, first, j))

    def sum_finish(held, into, name, first, last):
        span = pl.ds(first * share, (last - first) * share)
        for j in range(ways - 1):
            arrived(into.at[j, span], (name, first, j))
        values = []
        for i in range(first, last):
            value = held[pl.ds(pl.multiple_of(i * tok + way * share, share), share)]
            for j in range(ways - 1):
                value = value + into[j, i * share : (i + 1) * share].astype(F32)
            values.append(value)
        return values

    def send_ahead(k, value):
        ahead_out[k - 1] = value.astype(BF16)
        put(ahead_out.at[k - 1], ahead_in.at[k - 1], along(k), ("ahead", k))

    first_half, second_half = slice(0, half), slice(half, width)
    ga_halo.wait_near()
    bth_halo.wait_near()
    th1 = decay_through(bth, core + 1)
    early[0:tok] = ahead(1, None)
    early[tok : 2 * tok] = ahead(2, th1)
    sum_start(early, early_out, early_in, "early", 0, 2)
    send_far(groups - 1)
    ga_halo.finish()
    bth_halo.finish()
    fth_halo.finish()
    c_gather(4 + core, "far")
    arrived(bc.at[rows(1 - core)], ("c", "mate", "own"))
    arrived(bc.at[rows(3 - core)], ("c", "mate", "near"))
    near_adjoint[:, first_half] = adjoint_of(ga, 1) + th1[:, first_half] * adjoint_of(ga, 2)
    gb_halo.wait_near()
    near_adjoint[:, second_half] = adjoint_of(gb, 1) + th1[:, second_half] * adjoint_of(gb, 2)
    bth_halo.wait_far()
    th2 = th1 * decay_through(bth, core + 2)
    th3 = decay_through(bth, core + 3)
    ga_halo.wait_far()
    late[0:tok] = ahead(3, th2)
    late[tok : 2 * tok] = ahead(4, th2 * th3)
    sum_start(late, late_out, late_in, "late", 0, 2)
    ahead_1, ahead_2 = sum_finish(early, early_in, "early", 0, 2)
    send_ahead(1, ahead_1)
    send_ahead(2, ahead_2)
    for group in range(groups):
        send_near(group)
    x_halo.finish()
    arrived(bc.at[rows(5 - core)], ("c", "mate", "far"))

    def adjoint(ref, part):
        far = adjoint_of(ref, 3) + th3[:, part] * adjoint_of(ref, 4)
        return (near_adjoint[:, part] + th2[:, part] * far).astype(BF16)

    finish_input(first_half, adjoint(ga, first_half))
    ahead_3, ahead_4 = sum_finish(late, late_in, "late", 0, 2)
    send_ahead(3, ahead_3)
    send_ahead(4, ahead_4)
    gb_halo.finish()

    x_halo.wait_near()
    fth_halo.wait_near()
    fth_halo.wait_far()
    x_halo.wait_far()
    state_in = None
    for k in range(REACH, 0, -1):
        place = 4 + core - k
        value = dot(fx[rows(place), half:], fx[rows(place), 0:half], (0, 0))
        state_in = value if state_in is None else value + decay_through(fth, place)[:, half:] * state_in
    last[tok : 2 * tok] = last[tok : 2 * tok] + dot(gb[g_own], state_in.astype(BF16), (1, 1))
    sum_start(last, last_out, last_in, "last", 1, 2)
    gb_halo.wait_far()
    finish_input(second_half, adjoint(gb, second_half))
    sum_start(last, last_out, last_in, "last", 0, 1)
    for group in range(groups):
        finish_keys(group)
    (sum_c,) = sum_finish(last, last_in, "last", 1, 2)
    for k in range(1, REACH + 1):
        arrived(ahead_in.at[k - 1], ("ahead", k))
        sum_c = sum_c + ahead_in[k - 1].astype(F32)
    dc_ref[...] = sum_c.astype(BF16)
    (sum_b,) = sum_finish(last, last_in, "last", 0, 1)
    db_ref[...] = sum_b.astype(BF16)
    for one in started:
        one.wait_send()


def hand_over(*refs):
    count = len(refs) // 2
    for i in range(count):
        refs[count + i][...] = refs[i][...]


def solution(mesh):
    shards, ways = mesh.shape["ctx"], mesh.shape["head"]

    def on_device(queries, keys, values, grad_attn, ssm_input, ssm_b, ssm_c, log_decay, skip_gain, grad_ssm, doc_lengths):
        tok, kw = keys.shape
        width, state = ssm_input.shape[1], ssm_b.shape[1]
        ratio = queries.shape[1] // kw
        groups = kw // D_HEAD
        share = tok // ways
        vmem = pl.BlockSpec(memory_space=pltpu.VMEM)
        hbm = pl.BlockSpec(memory_space=pltpu.HBM)
        held = lambda a: pltpu.VMEM(a.shape, a.dtype)
        skips, lens = skip_gain.reshape(1, -1), doc_lengths.reshape(1, -1)
        shapes = [queries.shape, keys.shape, values.shape, ssm_input.shape, (share, state), (share, state)]
        results = pl.pallas_call(
            lambda *refs: kernel(shards, ways, *refs),
            out_shape=tuple(jax.ShapeDtypeStruct(shape, BF16) for shape in shapes),
            in_specs=[hbm] * 11,
            out_specs=(vmem,) * 6,
            scratch_shapes=[
                held(queries),
                held(grad_attn),
                held(ssm_input),
                held(ssm_b),
                held(log_decay),
                held(skips),
                held(grad_ssm),
                held(lens),
                pltpu.VMEM((groups, SLOTS * tok, 2 * D_HEAD), BF16),
                pltpu.VMEM((SLOTS * tok, width // 2 + state), BF16),
                pltpu.VMEM((SLOTS * 8, width // 8), F32),
                pltpu.VMEM((SLOTS * tok, width // 2), BF16),
                pltpu.VMEM((SLOTS * tok, width // 2), BF16),
                pltpu.VMEM((SLOTS * tok, state), BF16),
                pltpu.VMEM((SLOTS * 8, width // 8), F32),
                pltpu.VMEM((tok, width), BF16),
                pltpu.VMEM((groups, SLOTS * tok, 2 * D_HEAD), F32),
                pltpu.VMEM((groups, 3 * tok, 2 * D_HEAD), BF16),
                pltpu.VMEM((groups, 3 * tok, 2 * D_HEAD), BF16),
                pltpu.VMEM((groups, tok, 2 * D_HEAD), BF16),
                pltpu.VMEM((groups, tok, 2 * D_HEAD), BF16),
                pltpu.VMEM((groups, tok, 2 * D_HEAD), BF16),
                pltpu.VMEM((groups, tok, 2 * D_HEAD), BF16),
                pltpu.VMEM(((REACH + 1) * tok, ratio * tok), BF16),
                pltpu.VMEM(((REACH + 1) * tok, ratio * tok), BF16),
                pltpu.VMEM((tok, width), F32),
                pltpu.VMEM((tok, width), F32),
                pltpu.VMEM((state, width), F32),
                pltpu.VMEM((2 * tok, state), F32),
                pltpu.VMEM((ways, 2 * share, state), BF16),
                pltpu.VMEM((ways - 1, 2 * share, state), BF16),
                pltpu.VMEM((2 * tok, state), F32),
                pltpu.VMEM((ways, 2 * share, state), BF16),
                pltpu.VMEM((ways - 1, 2 * share, state), BF16),
                pltpu.VMEM((2 * tok, state), F32),
                pltpu.VMEM((ways, 2 * share, state), BF16),
                pltpu.VMEM((ways - 1, 2 * share, state), BF16),
                pltpu.VMEM((REACH, share, state), BF16),
                pltpu.VMEM((REACH, share, state), BF16),
                pltpu.SemaphoreType.DMA((TRANSFERS,)),
                pltpu.SemaphoreType.DMA((TRANSFERS,)),
                pltpu.SemaphoreType.DMA((9 + 2 * groups,)),
                pltpu.SemaphoreType.REGULAR,
            ],
            compiler_params=pltpu.CompilerParams(
                collective_id=0, has_side_effects=True, vmem_limit_bytes=VMEM_BYTES
            ),
        )(
            queries,
            keys,
            values,
            grad_attn,
            ssm_input,
            ssm_b,
            ssm_c,
            log_decay,
            skips,
            grad_ssm,
            lens,
        )
        return pl.pallas_call(
            hand_over,
            out_shape=tuple(jax.ShapeDtypeStruct(shape, BF16) for shape in shapes),
            in_specs=[vmem] * 6,
            out_specs=(vmem,) * 6,
        )(*results)

    both = P("ctx", "head")
    rows = P(("ctx", "head"), None)
    return jax.shard_map(
        on_device,
        mesh=mesh,
        in_specs=(both, both, both, both, both, P("ctx", None), P("ctx", None), P("head", "ctx"), P("head"), both, P()),
        out_specs=(both, both, both, both, rows, rows),
        check_vma=False,
    )
```

```python
import math

import jax
import jax.numpy as jnp
from jax import lax
from jax.experimental import pallas as pl
from jax.experimental.pallas import tpu as pltpu
from jax.sharding import PartitionSpec as P

D_HEAD = 128
MDIM = 64
REACH = 4
SLOTS = REACH + 2
TRANSFERS = 72
VMEM_BYTES = 56 * 1024 * 1024

F32 = jnp.float32
BF16 = jnp.bfloat16
MESH = pl.DeviceIdType.MESH
HIGH = lax.Precision.HIGHEST


def dot(a, b, over, precision=None):
    return lax.dot_general(
        a, b, ((over[:1], over[1:]), ((), ())), precision=precision, preferred_element_type=F32
    )


def iota(shape, dim):
    return lax.broadcasted_iota(jnp.int32, shape, dim)


def document_starts(lens, base, tok):
    docs = lens.shape[1]
    row, col = iota((docs, docs), 0), iota((docs, docs), 1)
    lens_row = jnp.broadcast_to(lens.astype(F32), (docs, docs))
    lens_col = jnp.sum(jnp.where(row == col, lens_row, 0.0), axis=1, keepdims=True)
    ends_col = jnp.sum(jnp.where(col <= row, lens_row, 0.0), axis=1, keepdims=True)
    ends_row = jnp.sum(jnp.where(row <= col, lens_col, 0.0), axis=0, keepdims=True)
    at_col = (base + iota((tok, docs), 0)).astype(F32)
    at_row = (base + iota((docs, tok), 1)).astype(F32)
    start_col = jnp.max(jnp.where(at_col >= ends_row, ends_row, 0.0), axis=1, keepdims=True)
    start_row = jnp.max(jnp.where(at_row >= ends_col, ends_col, 0.0), axis=0, keepdims=True)
    return start_col, start_row


def kernel(
    shards,
    ways,
    q_hbm,
    k_hbm,
    v_hbm,
    do_hbm,
    x_hbm,
    b_hbm,
    c_hbm,
    decay_hbm,
    skip_hbm,
    g_hbm,
    lens_hbm,
    dq_ref,
    dk_ref,
    dv_ref,
    dx_ref,
    db_ref,
    dc_ref,
    q_ref,
    do_ref,
    x_ref,
    b_ref,
    decay_ref,
    skip_ref,
    g_ref,
    lens_ref,
    kv,
    fx,
    fth,
    ga,
    gb,
    bc,
    bth,
    xs,
    dkv,
    mate_out,
    mate_in,
    far_out,
    far_in,
    near_out,
    near_in,
    probs,
    dscores,
    to_end,
    dx_acc,
    near_adjoint,
    early,
    early_out,
    early_in,
    late,
    late_out,
    late_in,
    last,
    last_out,
    last_in,
    ahead_out,
    ahead_in,
    send,
    recv,
    load,
    ready,
):
    tok, heads = q_ref.shape[0], decay_ref.shape[0]
    kw = k_hbm.shape[1]
    groups = kw // D_HEAD
    ratio = q_ref.shape[1] // kw
    width = x_ref.shape[1]
    share = tok // ways
    half = width // 2
    shard = lax.axis_index("ctx")
    way = lax.axis_index("head")
    core = lax.rem(shard, 2)

    def along(steps):
        return (lax.rem(shard + (steps + shards), shards), way)

    mate = (shard + 1 - 2 * core, way)
    up, down = along(2), along(-2)
    others = [(shard, lax.rem(way + j, ways)) for j in range(1, ways)]
    barrier = pltpu.get_barrier_semaphore()
    for peer in [along(-1), along(-2), mate] + others:
        pl.semaphore_signal(barrier, inc=1, device_id=peer, device_id_type=MESH)

    def rows(slot, size=tok):
        return pl.ds(pl.multiple_of(slot * size, size), size)

    numbers = {}

    def copy(source, target, peer, name):
        number = numbers.setdefault(name, len(numbers))
        return pltpu.make_async_remote_copy(
            src_ref=source,
            dst_ref=target,
            send_sem=send.at[number],
            recv_sem=recv.at[number],
            device_id=peer,
            device_id_type=MESH,
        )

    started = []

    def put(source, target, peer, name):
        one = copy(source, target, peer, name)
        one.start()
        started.append(one)

    def arrived(target, name):
        copy(target, target, mate, name).wait_recv()

    class Halo:
        def __init__(self, name, upward, view):
            self.name, self.view = name, view
            self.own, self.near, self.far = (4, 2, 0) if upward else (0, 2, 4)
            self.peer = up if upward else down

        def send(self, slot, peer, what, target=None):
            place = self.view(slot if target is None else target)
            put(self.view(slot), place, peer, (self.name, what))

        def begin(self):
            self.send(self.own + core, self.peer, "near", self.near + core)

        def begin_mate(self):
            self.send(self.own + core, mate, "mate own")

        def relay(self):
            arrived(self.view(self.near + core), (self.name, "near"))
            self.send(self.near + core, self.peer, "far", self.far + core)
            self.send(self.near + core, mate, "mate near")

        def finish(self):
            arrived(self.view(self.far + core), (self.name, "far"))
            self.send(self.far + core, mate, "mate far")

        def wait_near(self):
            arrived(self.view(self.own + 1 - core), (self.name, "mate own"))
            arrived(self.view(self.near + 1 - core), (self.name, "mate near"))

        def wait_far(self):
            arrived(self.view(self.far + 1 - core), (self.name, "mate far"))

    kv_halos = [Halo(("kv", i), True, lambda slot, i=i: kv.at[i, rows(slot)]) for i in range(groups)]
    x_halo = Halo("x", True, lambda slot: fx.at[rows(slot)])
    fth_halo = Halo("fth", True, lambda slot: fth.at[rows(slot, 8)])
    ga_halo = Halo("ga", False, lambda slot: ga.at[rows(slot)])
    gb_halo = Halo("gb", False, lambda slot: gb.at[rows(slot)])
    bth_halo = Halo("bth", False, lambda slot: bth.at[rows(slot, 8)])

    def c_part(slot, of):
        return bc.at[pl.ds(pl.multiple_of(slot * tok + of * share, share), share)]

    def c_spread(slot, name):
        for j, peer in enumerate(others):
            put(c_part(slot, way), c_part(slot, way), peer, ("c", name, j))

    def c_gather(slot, name):
        for j in range(ways - 1):
            arrived(c_part(slot, lax.rem(way + (ways - 1 - j), ways)), ("c", name, j))
        put(bc.at[rows(slot)], bc.at[rows(slot)], mate, ("c", "mate", name))

    own = rows(4 + core)
    g_own = rows(core)
    loads = {}
    places = [
        ("lens", lens_hbm, lens_ref),
        ("decay", decay_hbm, decay_ref),
        ("skip", skip_hbm, skip_ref),
    ]
    for i in range(groups):
        part_of = slice(i * D_HEAD, (i + 1) * D_HEAD)
        places.append(("k", k_hbm.at[:, part_of], kv.at[i, own, 0:D_HEAD]))
        places.append(("v", v_hbm.at[:, part_of], kv.at[i, own, D_HEAD : 2 * D_HEAD]))
    places += [
        ("c", c_hbm, bc.at[g_own]),
        ("g", g_hbm, g_ref),
        ("x", x_hbm, x_ref),
        ("b", b_hbm, b_ref),
        ("q", q_hbm, q_ref),
        ("do", do_hbm, do_ref),
    ]
    for number, (name, source, target) in enumerate(places):
        one = pltpu.make_async_copy(source, target, load.at[number])
        one.start()
        loads.setdefault(name, []).append(one)

    def loaded(*names):
        for name in names:
            for one in loads[name]:
                one.wait()

    def pieces(value):
        high = value.astype(BF16)
        middle = (value - high.astype(F32)).astype(BF16)
        return high, middle, (value - high.astype(F32) - middle.astype(F32)).astype(BF16)

    def widen(value, count):
        return sum(dot(piece, spread, (1, 0)) for piece in pieces(value)[:count])

    pl.semaphore_wait(barrier, 3 + len(others))
    pl.semaphore_signal(ready, inc=1, device_id=up, device_id_type=MESH)
    loaded("k", "v")
    for halo in kv_halos:
        halo.begin()
    for halo in kv_halos:
        halo.begin_mate()
    loaded("lens", "decay", "skip")
    base = shard * tok
    base_f = base.astype(F32)
    start_col, start_row = document_starts(lens_ref[...], base, tok)
    later = (iota((tok, tok), 0) >= iota((tok, tok), 1)).astype(BF16)
    decay_pieces = pieces(decay_ref[...])
    cum_col = sum(dot(later, piece, (1, 1)) for piece in decay_pieces)
    carried = jnp.exp(cum_col) * (start_col < base_f).astype(F32)
    spread = (iota((heads, width), 1) // MDIM == iota((heads, width), 0)).astype(BF16)
    total = cum_col[tok - 1 : tok, :]
    last_start = start_col[tok - 1 : tok, :]
    through = jnp.exp(total) * (last_start < base_f).astype(F32)
    table = jnp.concatenate([jnp.broadcast_to(through, (8, heads)), jnp.broadcast_to(skip_ref[...], (8, heads))], axis=0)
    wide = widen(table, 3)
    skip = wide[8:9]
    th = jnp.concatenate([wide[0:1, i * (width // 8) : (i + 1) * (width // 8)] for i in range(8)], axis=0)
    bth[rows(core, 8)] = th
    fth[rows(4 + core, 8)] = th
    fth_halo.begin()
    wide = widen(carried, 2)
    loaded("g", "c")
    ga[g_own] = (g_ref[:, 0:half].astype(F32) * wide[:, 0:half]).astype(BF16)
    gb[g_own] = (g_ref[:, half:].astype(F32) * wide[:, half:]).astype(BF16)
    pl.semaphore_wait(ready, 1)
    put(c_part(core, way), c_part(2 + core, way), down, ("c", "near"))
    bth_halo.begin()
    ga_halo.begin()
    gb_halo.begin()
    to_end[...] = widen(jnp.exp(total - cum_col) * (start_col == last_start).astype(F32), 2)
    loaded("x", "b")
    xs[...] = (x_ref[...].astype(F32) * to_end[...]).astype(BF16)
    fx[own, 0:half] = xs[:, half:]
    fx[own, half:] = b_ref[...]
    for halo in (fth_halo, bth_halo, ga_halo, gb_halo, x_halo):
        halo.begin_mate()
    put(bc.at[g_own], bc.at[g_own], mate, ("c", "mate", "own"))
    cum_row = sum(dot(piece, later, (1, 1)) for piece in decay_pieces)
    state = dot(b_ref[...], xs[:, 0:half], (0, 0))

    causal = (iota((tok, tok), 0) >= iota((tok, tok), 1)) & (
        start_col <= (base + iota((tok, tok), 1)).astype(F32)
    )
    couple = dot(bc[g_own], b_ref[...], (1, 1))
    low = iota((tok, 2 * MDIM), 1) < MDIM

    def pair_of_heads(pair, mix):
        part = slice(pair * 2 * MDIM, (pair + 1) * 2 * MDIM)
        grad = g_ref[:, part]
        none = jnp.zeros_like(grad)
        both = jnp.concatenate([jnp.where(low, grad, none), jnp.where(low, none, grad)], axis=0)
        pairs = dot(both, x_ref[:, part], (1, 1))
        within = [
            jnp.exp(jnp.where(causal, cum_col[:, h : h + 1] - cum_row[h : h + 1, :], -1e30))
            for h in (2 * pair, 2 * pair + 1)
        ]
        back = jnp.concatenate([w * couple for w in within], axis=0).astype(BF16)
        dx_acc[:, part] = dot(back, both, (0, 0))
        return mix + pairs[0:tok] * within[0] + pairs[tok : 2 * tok] * within[1]

    mix = jnp.zeros((tok, tok), F32)
    for pair in range(heads // 4):
        mix = pair_of_heads(pair, mix)
    kv_halos[0].relay()
    for pair in range(heads // 4, heads // 2 - 2):
        mix = pair_of_heads(pair, mix)
    for halo in kv_halos[1:]:
        halo.relay()
    x_halo.begin()
    for pair in range(heads // 2 - 2, heads // 2):
        mix = pair_of_heads(pair, mix)
    mix = mix.astype(BF16)
    last[0:tok] = dot(mix, bc[g_own], (0, 0))
    last[tok : 2 * tok] = dot(mix, b_ref[...], (1, 0))
    arrived(c_part(2 + core, way), ("c", "near"))
    put(c_part(2 + core, way), c_part(4 + core, way), down, ("c", "far"))
    c_spread(2 + core, "near")
    bth_halo.relay()
    fth_halo.relay()
    kv_halos[0].finish()
    ga_halo.relay()
    kv_halos[1].finish()

    loaded("q", "do")
    window = (REACH + 1) * tok
    seen = pl.ds(pl.multiple_of(core * tok, tok), window)
    key_at = (base - REACH * tok + iota((window, tok), 0)).astype(F32)
    query_at = (base + iota((window, tok), 1)).astype(F32)
    allowed = (key_at <= query_at) & (key_at >= start_row)
    bias = jnp.where(allowed, 0.0, -1e30)
    bias = jnp.concatenate([bias, bias], axis=1)
    scale = 1.0 / math.sqrt(D_HEAD)
    idle = rows(5 * (1 - core))

    def attend(group):
        keys = kv[group, seen, 0:D_HEAD]
        values = kv[group, seen, D_HEAD : 2 * D_HEAD]
        heads_of = [slice((group * ratio + r) * D_HEAD, (group * ratio + r + 1) * D_HEAD) for r in range(ratio)]
        queries = jnp.concatenate([q_ref[:, part] for part in heads_of], axis=0)
        outgrad = jnp.concatenate([do_ref[:, part] for part in heads_of], axis=0)
        for half in range(ratio // 2):
            part = slice(half * 2 * tok, (half + 1) * 2 * tok)
            scores = dot(keys, queries[part], (1, 1)) * scale + bias
            weights = jnp.exp(scores - jnp.max(scores, axis=0, keepdims=True))
            normed = weights * (1.0 / jnp.sum(weights, axis=0, keepdims=True))
            dprobs = dot(values, outgrad[part], (1, 1))
            centre = jnp.sum(normed * dprobs, axis=0, keepdims=True)
            probs[:, part] = normed.astype(BF16)
            dscores[:, part] = (normed * (dprobs - centre)).astype(BF16)
        dkv[group, idle] = jnp.zeros((tok, 2 * D_HEAD), F32)
        dkv[group, seen, 0:D_HEAD] = dot(dscores[...], queries, (1, 0)) * scale
        dkv[group, seen, D_HEAD : 2 * D_HEAD] = dot(probs[...], outgrad, (1, 0))
        for i in range(3):
            mate_out[group, rows(i)] = dkv[group, rows(2 * i + 1 - core)].astype(BF16)
        put(mate_out.at[group], mate_in.at[group], mate, ("dkv mate", group))
        grad_query = dot(dscores[...], keys, (0, 0)) * scale
        for r, part in enumerate(heads_of):
            dq_ref[:, part] = grad_query[r * tok : (r + 1) * tok].astype(BF16)

    def send_far(group):
        arrived(mate_in.at[group], ("dkv mate", group))
        far_out[group] = (dkv[group, rows(core)] + mate_in[group, rows(0)].astype(F32)).astype(BF16)
        put(far_out.at[group], far_in.at[group], down, ("dkv far", group))

    def send_near(group):
        arrived(far_in.at[group], ("dkv far", group))
        near = dkv[group, rows(2 + core)] + mate_in[group, rows(1)].astype(F32) + far_in[group].astype(F32)
        near_out[group] = near.astype(BF16)
        put(near_out.at[group], near_in.at[group], down, ("dkv near", group))

    def finish_keys(group):
        arrived(near_in.at[group], ("dkv near", group))
        total_kv = dkv[group, rows(4 + core)] + mate_in[group, rows(2)].astype(F32) + near_in[group].astype(F32)
        part = slice(group * D_HEAD, (group + 1) * D_HEAD)
        dk_ref[:, part] = total_kv[:, 0:D_HEAD].astype(BF16)
        dv_ref[:, part] = total_kv[:, D_HEAD : 2 * D_HEAD].astype(BF16)

    for group in range(groups):
        kv_halos[group].wait_near()
        kv_halos[group].wait_far()
        attend(group)
        if group == 0:
            gb_halo.relay()
            x_halo.relay()
            arrived(c_part(4 + core, way), ("c", "far"))
            c_spread(4 + core, "far")
            c_gather(2 + core, "near")
        else:
            send_far(group - 1)

    def decay_through(ths, slot):
        row = ths[rows(slot, 8)]
        return jnp.concatenate([row[i : i + 1] for i in range(8)], axis=1)

    def adjoint_of(ref, k):
        return dot(bc[rows(core + k)], ref[rows(core + k)], (0, 0))

    def ahead(k, factor):
        value = state if factor is None else state * factor[:, 0:half]
        return dot(ga[rows(core + k)], value.astype(BF16), (1, 1))

    def finish_input(part, adjoint):
        last[0:tok] = last[0:tok] + dot(xs[:, part], adjoint, (1, 1))
        dx = dx_acc[:, part] + dot(b_ref[...], adjoint, (1, 0)) * to_end[:, part]
        dx_ref[:, part] = (dx + skip[:, part] * g_ref[:, part].astype(F32)).astype(BF16)

    def sum_start(held, out, into, name, first, last):
        span = pl.ds(first * share, (last - first) * share)
        for j in range(ways):
            for i in range(first, last):
                part = held[i * tok + j * share : i * tok + (j + 1) * share]
                out[j, i * share : (i + 1) * share] = part.astype(BF16)
        for j, peer in enumerate(others):
            put(out.at[peer[1], span], into.at[j, span], peer, (name, first, j))

    def sum_finish(held, into, name, first, last):
        span = pl.ds(first * share, (last - first) * share)
        for j in range(ways - 1):
            arrived(into.at[j, span], (name, first, j))
        values = []
        for i in range(first, last):
            value = held[pl.ds(pl.multiple_of(i * tok + way * share, share), share)]
            for j in range(ways - 1):
                value = value + into[j, i * share : (i + 1) * share].astype(F32)
            values.append(value)
        return values

    def send_ahead(k, value):
        ahead_out[k - 1] = value.astype(BF16)
        put(ahead_out.at[k - 1], ahead_in.at[k - 1], along(k), ("ahead", k))

    first_half, second_half = slice(0, half), slice(half, width)
    ga_halo.wait_near()
    bth_halo.wait_near()
    th1 = decay_through(bth, core + 1)
    early[0:tok] = ahead(1, None)
    early[tok : 2 * tok] = ahead(2, th1)
    sum_start(early, early_out, early_in, "early", 0, 2)
    ga_halo.finish()
    bth_halo.finish()
    send_far(groups - 1)
    bth_halo.wait_far()
    th2 = th1 * decay_through(bth, core + 2)
    th3 = decay_through(bth, core + 3)
    ga_halo.wait_far()
    late[0:tok] = ahead(3, th2)
    late[tok : 2 * tok] = ahead(4, th2 * th3)
    sum_start(late, late_out, late_in, "late", 0, 2)
    x_halo.finish()
    fth_halo.finish()
    gb_halo.finish()
    c_gather(4 + core, "far")
    arrived(bc.at[rows(1 - core)], ("c", "mate", "own"))
    arrived(bc.at[rows(3 - core)], ("c", "mate", "near"))
    near_adjoint[:, first_half] = adjoint_of(ga, 1) + th1[:, first_half] * adjoint_of(ga, 2)
    gb_halo.wait_near()
    near_adjoint[:, second_half] = adjoint_of(gb, 1) + th1[:, second_half] * adjoint_of(gb, 2)
    ahead_1, ahead_2 = sum_finish(early, early_in, "early", 0, 2)
    send_ahead(1, ahead_1)
    send_ahead(2, ahead_2)
    for group in range(groups):
        send_near(group)
    arrived(bc.at[rows(5 - core)], ("c", "mate", "far"))

    def adjoint(ref, part):
        far = adjoint_of(ref, 3) + th3[:, part] * adjoint_of(ref, 4)
        return (near_adjoint[:, part] + th2[:, part] * far).astype(BF16)

    finish_input(first_half, adjoint(ga, first_half))
    ahead_3, ahead_4 = sum_finish(late, late_in, "late", 0, 2)
    send_ahead(3, ahead_3)
    send_ahead(4, ahead_4)

    x_halo.wait_near()
    fth_halo.wait_near()
    fth_halo.wait_far()
    x_halo.wait_far()
    state_in = None
    for k in range(REACH, 0, -1):
        place = 4 + core - k
        value = dot(fx[rows(place), half:], fx[rows(place), 0:half], (0, 0))
        state_in = value if state_in is None else value + decay_through(fth, place)[:, half:] * state_in
    last[tok : 2 * tok] = last[tok : 2 * tok] + dot(gb[g_own], state_in.astype(BF16), (1, 1))
    sum_start(last, last_out, last_in, "last", 1, 2)
    gb_halo.wait_far()
    finish_input(second_half, adjoint(gb, second_half))
    sum_start(last, last_out, last_in, "last", 0, 1)
    for group in range(groups):
        finish_keys(group)
    (sum_c,) = sum_finish(last, last_in, "last", 1, 2)
    for k in range(1, REACH + 1):
        arrived(ahead_in.at[k - 1], ("ahead", k))
        sum_c = sum_c + ahead_in[k - 1].astype(F32)
    dc_ref[...] = sum_c.astype(BF16)
    (sum_b,) = sum_finish(last, last_in, "last", 0, 1)
    db_ref[...] = sum_b.astype(BF16)
    for one in started:
        one.wait_send()


def hand_over(*refs):
    count = len(refs) // 2
    for i in range(count):
        refs[count + i][...] = refs[i][...]


def solution(mesh):
    shards, ways = mesh.shape["ctx"], mesh.shape["head"]

    def on_device(queries, keys, values, grad_attn, ssm_input, ssm_b, ssm_c, log_decay, skip_gain, grad_ssm, doc_lengths):
        tok, kw = keys.shape
        width, state = ssm_input.shape[1], ssm_b.shape[1]
        ratio = queries.shape[1] // kw
        groups = kw // D_HEAD
        share = tok // ways
        vmem = pl.BlockSpec(memory_space=pltpu.VMEM)
        hbm = pl.BlockSpec(memory_space=pltpu.HBM)
        held = lambda a: pltpu.VMEM(a.shape, a.dtype)
        skips, lens = skip_gain.reshape(1, -1), doc_lengths.reshape(1, -1)
        shapes = [queries.shape, keys.shape, values.shape, ssm_input.shape, (share, state), (share, state)]
        results = pl.pallas_call(
            lambda *refs: kernel(shards, ways, *refs),
            out_shape=tuple(pltpu.VMEM(shape, BF16) for shape in shapes),
            in_specs=[hbm] * 11,
            out_specs=(vmem,) * 6,
            scratch_shapes=[
                held(queries),
                held(grad_attn),
                held(ssm_input),
                held(ssm_b),
                held(log_decay),
                held(skips),
                held(grad_ssm),
                held(lens),
                pltpu.VMEM((groups, SLOTS * tok, 2 * D_HEAD), BF16),
                pltpu.VMEM((SLOTS * tok, width // 2 + state), BF16),
                pltpu.VMEM((SLOTS * 8, width // 8), F32),
                pltpu.VMEM((SLOTS * tok, width // 2), BF16),
                pltpu.VMEM((SLOTS * tok, width // 2), BF16),
                pltpu.VMEM((SLOTS * tok, state), BF16),
                pltpu.VMEM((SLOTS * 8, width // 8), F32),
                pltpu.VMEM((tok, width), BF16),
                pltpu.VMEM((groups, SLOTS * tok, 2 * D_HEAD), F32),
                pltpu.VMEM((groups, 3 * tok, 2 * D_HEAD), BF16),
                pltpu.VMEM((groups, 3 * tok, 2 * D_HEAD), BF16),
                pltpu.VMEM((groups, tok, 2 * D_HEAD), BF16),
                pltpu.VMEM((groups, tok, 2 * D_HEAD), BF16),
                pltpu.VMEM((groups, tok, 2 * D_HEAD), BF16),
                pltpu.VMEM((groups, tok, 2 * D_HEAD), BF16),
                pltpu.VMEM(((REACH + 1) * tok, ratio * tok), BF16),
                pltpu.VMEM(((REACH + 1) * tok, ratio * tok), BF16),
                pltpu.VMEM((tok, width), F32),
                pltpu.VMEM((tok, width), F32),
                pltpu.VMEM((state, width), F32),
                pltpu.VMEM((2 * tok, state), F32),
                pltpu.VMEM((ways, 2 * share, state), BF16),
                pltpu.VMEM((ways - 1, 2 * share, state), BF16),
                pltpu.VMEM((2 * tok, state), F32),
                pltpu.VMEM((ways, 2 * share, state), BF16),
                pltpu.VMEM((ways - 1, 2 * share, state), BF16),
                pltpu.VMEM((2 * tok, state), F32),
                pltpu.VMEM((ways, 2 * share, state), BF16),
                pltpu.VMEM((ways - 1, 2 * share, state), BF16),
                pltpu.VMEM((REACH, share, state), BF16),
                pltpu.VMEM((REACH, share, state), BF16),
                pltpu.SemaphoreType.DMA((TRANSFERS,)),
                pltpu.SemaphoreType.DMA((TRANSFERS,)),
                pltpu.SemaphoreType.DMA((9 + 2 * groups,)),
                pltpu.SemaphoreType.REGULAR,
            ],
            compiler_params=pltpu.CompilerParams(
                collective_id=0, has_side_effects=True, vmem_limit_bytes=VMEM_BYTES
            ),
        )(
            queries,
            keys,
            values,
            grad_attn,
            ssm_input,
            ssm_b,
            ssm_c,
            log_decay,
            skips,
            grad_ssm,
            lens,
        )
        return pl.pallas_call(
            hand_over,
            out_shape=tuple(jax.ShapeDtypeStruct(shape, BF16) for shape in shapes),
            in_specs=[vmem] * 6,
            out_specs=(vmem,) * 6,
            compiler_params=pltpu.CompilerParams(vmem_limit_bytes=4 * 1024 * 1024),
        )(*results)

    both = P("ctx", "head")
    rows = P(("ctx", "head"), None)
    return jax.shard_map(
        on_device,
        mesh=mesh,
        in_specs=(both, both, both, both, both, P("ctx", None), P("ctx", None), P("head", "ctx"), P("head"), both, P()),
        out_specs=(both, both, both, both, rows, rows),
        check_vma=False,
    )
```

```python
import math

import jax
import jax.numpy as jnp
from jax import lax
from jax.experimental import pallas as pl
from jax.experimental.pallas import tpu as pltpu
from jax.sharding import PartitionSpec as P

D_HEAD = 128
MDIM = 64
REACH = 4
SLOTS = REACH + 2
EIGHTHS = 5
TRANSFERS = 72
VMEM_BYTES = 56 * 1024 * 1024

F32 = jnp.float32
BF16 = jnp.bfloat16
MESH = pl.DeviceIdType.MESH
HIGH = lax.Precision.HIGHEST


def dot(a, b, over, precision=None):
    return lax.dot_general(
        a, b, ((over[:1], over[1:]), ((), ())), precision=precision, preferred_element_type=F32
    )


def iota(shape, dim):
    return lax.broadcasted_iota(jnp.int32, shape, dim)


def document_starts(lens, base, tok):
    docs = lens.shape[1]
    row, col = iota((docs, docs), 0), iota((docs, docs), 1)
    lens_row = jnp.broadcast_to(lens.astype(F32), (docs, docs))
    lens_col = jnp.sum(jnp.where(row == col, lens_row, 0.0), axis=1, keepdims=True)
    ends_col = jnp.sum(jnp.where(col <= row, lens_row, 0.0), axis=1, keepdims=True)
    ends_row = jnp.sum(jnp.where(row <= col, lens_col, 0.0), axis=0, keepdims=True)
    at_col = (base + iota((tok, docs), 0)).astype(F32)
    at_row = (base + iota((docs, tok), 1)).astype(F32)
    start_col = jnp.max(jnp.where(at_col >= ends_row, ends_row, 0.0), axis=1, keepdims=True)
    start_row = jnp.max(jnp.where(at_row >= ends_col, ends_col, 0.0), axis=0, keepdims=True)
    return start_col, start_row


def kernel(
    shards,
    ways,
    q_hbm,
    k_hbm,
    v_hbm,
    do_hbm,
    x_hbm,
    b_hbm,
    c_hbm,
    decay_hbm,
    skip_hbm,
    g_hbm,
    lens_hbm,
    dq_ref,
    dk_ref,
    dv_ref,
    dx_ref,
    db_ref,
    dc_ref,
    q_ref,
    do_ref,
    x_ref,
    b_ref,
    decay_ref,
    skip_ref,
    g_ref,
    lens_ref,
    kv,
    fx,
    fth,
    ga,
    gb,
    bc,
    bth,
    xs,
    dkv,
    mate_out,
    mate_in,
    far_out,
    far_in,
    near_out,
    near_in,
    probs,
    dscores,
    to_end,
    dx_acc,
    near_adjoint,
    early,
    early_out,
    early_in,
    late,
    late_out,
    late_in,
    last,
    last_out,
    last_in,
    ahead_out,
    ahead_in,
    send,
    recv,
    load,
    ready,
):
    tok, heads = q_ref.shape[0], decay_ref.shape[0]
    kw = k_hbm.shape[1]
    groups = kw // D_HEAD
    ratio = q_ref.shape[1] // kw
    width = x_ref.shape[1]
    share = tok // ways
    half = width // 8 * EIGHTHS
    rest = width - half
    shard = lax.axis_index("ctx")
    way = lax.axis_index("head")
    core = lax.rem(shard, 2)

    def along(steps):
        return (lax.rem(shard + (steps + shards), shards), way)

    mate = (shard + 1 - 2 * core, way)
    up, down = along(2), along(-2)
    others = [(shard, lax.rem(way + j, ways)) for j in range(1, ways)]
    barrier = pltpu.get_barrier_semaphore()
    for peer in [along(-1), along(-2), mate] + others:
        pl.semaphore_signal(barrier, inc=1, device_id=peer, device_id_type=MESH)

    def rows(slot, size=tok):
        return pl.ds(pl.multiple_of(slot * size, size), size)

    numbers = {}

    def copy(source, target, peer, name):
        number = numbers.setdefault(name, len(numbers))
        return pltpu.make_async_remote_copy(
            src_ref=source,
            dst_ref=target,
            send_sem=send.at[number],
            recv_sem=recv.at[number],
            device_id=peer,
            device_id_type=MESH,
        )

    started = []

    def put(source, target, peer, name):
        one = copy(source, target, peer, name)
        one.start()
        started.append(one)

    def arrived(target, name):
        copy(target, target, mate, name).wait_recv()

    class Halo:
        def __init__(self, name, upward, view):
            self.name, self.view = name, view
            self.own, self.near, self.far = (4, 2, 0) if upward else (0, 2, 4)
            self.peer = up if upward else down

        def send(self, slot, peer, what, target=None):
            place = self.view(slot if target is None else target)
            put(self.view(slot), place, peer, (self.name, what))

        def begin(self):
            self.send(self.own + core, self.peer, "near", self.near + core)

        def begin_mate(self):
            self.send(self.own + core, mate, "mate own")

        def relay(self):
            arrived(self.view(self.near + core), (self.name, "near"))
            self.send(self.near + core, self.peer, "far", self.far + core)
            self.send(self.near + core, mate, "mate near")

        def finish(self):
            arrived(self.view(self.far + core), (self.name, "far"))
            self.send(self.far + core, mate, "mate far")

        def wait_near(self):
            arrived(self.view(self.own + 1 - core), (self.name, "mate own"))
            arrived(self.view(self.near + 1 - core), (self.name, "mate near"))

        def wait_far(self):
            arrived(self.view(self.far + 1 - core), (self.name, "mate far"))

    kv_halos = [Halo(("kv", i), True, lambda slot, i=i: kv.at[i, rows(slot)]) for i in range(groups)]
    x_halo = Halo("x", True, lambda slot: fx.at[rows(slot)])
    fth_halo = Halo("fth", True, lambda slot: fth.at[rows(slot, 8)])
    ga_halo = Halo("ga", False, lambda slot: ga.at[rows(slot)])
    gb_halo = Halo("gb", False, lambda slot: gb.at[rows(slot)])
    bth_halo = Halo("bth", False, lambda slot: bth.at[rows(slot, 8)])

    def c_part(slot, of):
        return bc.at[pl.ds(pl.multiple_of(slot * tok + of * share, share), share)]

    def c_spread(slot, name):
        for j, peer in enumerate(others):
            put(c_part(slot, way), c_part(slot, way), peer, ("c", name, j))

    def c_gather(slot, name):
        for j in range(ways - 1):
            arrived(c_part(slot, lax.rem(way + (ways - 1 - j), ways)), ("c", name, j))
        put(bc.at[rows(slot)], bc.at[rows(slot)], mate, ("c", "mate", name))

    own = rows(4 + core)
    g_own = rows(core)
    loads = {}
    places = [
        ("lens", lens_hbm, lens_ref),
        ("decay", decay_hbm, decay_ref),
        ("skip", skip_hbm, skip_ref),
    ]
    for i in range(groups):
        part_of = slice(i * D_HEAD, (i + 1) * D_HEAD)
        places.append(("k", k_hbm.at[:, part_of], kv.at[i, own, 0:D_HEAD]))
        places.append(("v", v_hbm.at[:, part_of], kv.at[i, own, D_HEAD : 2 * D_HEAD]))
    places += [
        ("c", c_hbm, bc.at[g_own]),
        ("g", g_hbm, g_ref),
        ("x", x_hbm, x_ref),
        ("b", b_hbm, b_ref),
        ("q", q_hbm, q_ref),
        ("do", do_hbm, do_ref),
    ]
    for number, (name, source, target) in enumerate(places):
        one = pltpu.make_async_copy(source, target, load.at[number])
        one.start()
        loads.setdefault(name, []).append(one)

    def loaded(*names):
        for name in names:
            for one in loads[name]:
                one.wait()

    def pieces(value):
        high = value.astype(BF16)
        middle = (value - high.astype(F32)).astype(BF16)
        return high, middle, (value - high.astype(F32) - middle.astype(F32)).astype(BF16)

    def widen(value, count):
        return sum(dot(piece, spread, (1, 0)) for piece in pieces(value)[:count])

    pl.semaphore_wait(barrier, 3 + len(others))
    pl.semaphore_signal(ready, inc=1, device_id=up, device_id_type=MESH)
    loaded("k", "v")
    for halo in kv_halos:
        halo.begin()
    for halo in kv_halos:
        halo.begin_mate()
    loaded("lens", "decay", "skip")
    base = shard * tok
    base_f = base.astype(F32)
    start_col, start_row = document_starts(lens_ref[...], base, tok)
    later = (iota((tok, tok), 0) >= iota((tok, tok), 1)).astype(BF16)
    decay_pieces = pieces(decay_ref[...])
    cum_col = sum(dot(later, piece, (1, 1)) for piece in decay_pieces)
    carried = jnp.exp(cum_col) * (start_col < base_f).astype(F32)
    spread = (iota((heads, width), 1) // MDIM == iota((heads, width), 0)).astype(BF16)
    total = cum_col[tok - 1 : tok, :]
    last_start = start_col[tok - 1 : tok, :]
    through = jnp.exp(total) * (last_start < base_f).astype(F32)
    table = jnp.concatenate([jnp.broadcast_to(through, (8, heads)), jnp.broadcast_to(skip_ref[...], (8, heads))], axis=0)
    wide = widen(table, 3)
    skip = wide[8:9]
    th = jnp.concatenate([wide[0:1, i * (width // 8) : (i + 1) * (width // 8)] for i in range(8)], axis=0)
    bth[rows(core, 8)] = th
    fth[rows(4 + core, 8)] = th
    fth_halo.begin()
    wide = widen(carried, 2)
    loaded("g", "c")
    ga[g_own] = (g_ref[:, 0:half].astype(F32) * wide[:, 0:half]).astype(BF16)
    gb[g_own] = (g_ref[:, half:].astype(F32) * wide[:, half:]).astype(BF16)
    pl.semaphore_wait(ready, 1)
    put(c_part(core, way), c_part(2 + core, way), down, ("c", "near"))
    bth_halo.begin()
    ga_halo.begin()
    gb_halo.begin()
    to_end[...] = widen(jnp.exp(total - cum_col) * (start_col == last_start).astype(F32), 2)
    loaded("x", "b")
    xs[...] = (x_ref[...].astype(F32) * to_end[...]).astype(BF16)
    fx[own, 0:rest] = xs[:, half:]
    fx[own, rest:] = b_ref[...]
    for halo in (fth_halo, bth_halo, ga_halo, gb_halo, x_halo):
        halo.begin_mate()
    put(bc.at[g_own], bc.at[g_own], mate, ("c", "mate", "own"))
    cum_row = sum(dot(piece, later, (1, 1)) for piece in decay_pieces)
    state = dot(b_ref[...], xs[:, 0:half], (0, 0))

    causal = (iota((tok, tok), 0) >= iota((tok, tok), 1)) & (
        start_col <= (base + iota((tok, tok), 1)).astype(F32)
    )
    couple = dot(bc[g_own], b_ref[...], (1, 1))
    low = iota((tok, 2 * MDIM), 1) < MDIM

    def pair_of_heads(pair, mix):
        part = slice(pair * 2 * MDIM, (pair + 1) * 2 * MDIM)
        grad = g_ref[:, part]
        none = jnp.zeros_like(grad)
        both = jnp.concatenate([jnp.where(low, grad, none), jnp.where(low, none, grad)], axis=0)
        pairs = dot(both, x_ref[:, part], (1, 1))
        within = [
            jnp.exp(jnp.where(causal, cum_col[:, h : h + 1] - cum_row[h : h + 1, :], -1e30))
            for h in (2 * pair, 2 * pair + 1)
        ]
        back = jnp.concatenate([w * couple for w in within], axis=0).astype(BF16)
        dx_acc[:, part] = dot(back, both, (0, 0))
        return mix + pairs[0:tok] * within[0] + pairs[tok : 2 * tok] * within[1]

    mix = jnp.zeros((tok, tok), F32)
    for pair in range(heads // 4):
        mix = pair_of_heads(pair, mix)
    kv_halos[0].relay()
    for pair in range(heads // 4, heads // 2 - 2):
        mix = pair_of_heads(pair, mix)
    for halo in kv_halos[1:]:
        halo.relay()
    x_halo.begin()
    for pair in range(heads // 2 - 2, heads // 2):
        mix = pair_of_heads(pair, mix)
    mix = mix.astype(BF16)
    last[0:tok] = dot(mix, bc[g_own], (0, 0))
    last[tok : 2 * tok] = dot(mix, b_ref[...], (1, 0))
    arrived(c_part(2 + core, way), ("c", "near"))
    put(c_part(2 + core, way), c_part(4 + core, way), down, ("c", "far"))
    c_spread(2 + core, "near")
    bth_halo.relay()
    fth_halo.relay()
    kv_halos[0].finish()
    ga_halo.relay()
    kv_halos[1].finish()

    loaded("q", "do")
    window = (REACH + 1) * tok
    seen = pl.ds(pl.multiple_of(core * tok, tok), window)
    key_at = (base - REACH * tok + iota((window, tok), 0)).astype(F32)
    query_at = (base + iota((window, tok), 1)).astype(F32)
    allowed = (key_at <= query_at) & (key_at >= start_row)
    bias = jnp.where(allowed, 0.0, -1e30)
    bias = jnp.concatenate([bias, bias], axis=1)
    scale = 1.0 / math.sqrt(D_HEAD)
    idle = rows(5 * (1 - core))

    def attend(group):
        keys = kv[group, seen, 0:D_HEAD]
        values = kv[group, seen, D_HEAD : 2 * D_HEAD]
        heads_of = [slice((group * ratio + r) * D_HEAD, (group * ratio + r + 1) * D_HEAD) for r in range(ratio)]
        queries = jnp.concatenate([q_ref[:, part] for part in heads_of], axis=0)
        outgrad = jnp.concatenate([do_ref[:, part] for part in heads_of], axis=0)
        for half in range(ratio // 2):
            part = slice(half * 2 * tok, (half + 1) * 2 * tok)
            scores = dot(keys, queries[part], (1, 1)) * scale + bias
            weights = jnp.exp(scores - jnp.max(scores, axis=0, keepdims=True))
            normed = weights * (1.0 / jnp.sum(weights, axis=0, keepdims=True))
            dprobs = dot(values, outgrad[part], (1, 1))
            centre = jnp.sum(normed * dprobs, axis=0, keepdims=True)
            probs[:, part] = normed.astype(BF16)
            dscores[:, part] = (normed * (dprobs - centre)).astype(BF16)
        dkv[group, idle] = jnp.zeros((tok, 2 * D_HEAD), F32)
        dkv[group, seen, 0:D_HEAD] = dot(dscores[...], queries, (1, 0)) * scale
        dkv[group, seen, D_HEAD : 2 * D_HEAD] = dot(probs[...], outgrad, (1, 0))
        for i in range(3):
            mate_out[group, rows(i)] = dkv[group, rows(2 * i + 1 - core)].astype(BF16)
        put(mate_out.at[group], mate_in.at[group], mate, ("dkv mate", group))
        grad_query = dot(dscores[...], keys, (0, 0)) * scale
        for r, part in enumerate(heads_of):
            dq_ref[:, part] = grad_query[r * tok : (r + 1) * tok].astype(BF16)

    def send_far(group):
        arrived(mate_in.at[group], ("dkv mate", group))
        far_out[group] = (dkv[group, rows(core)] + mate_in[group, rows(0)].astype(F32)).astype(BF16)
        put(far_out.at[group], far_in.at[group], down, ("dkv far", group))

    def send_near(group):
        arrived(far_in.at[group], ("dkv far", group))
        near = dkv[group, rows(2 + core)] + mate_in[group, rows(1)].astype(F32) + far_in[group].astype(F32)
        near_out[group] = near.astype(BF16)
        put(near_out.at[group], near_in.at[group], down, ("dkv near", group))

    def finish_keys(group):
        arrived(near_in.at[group], ("dkv near", group))
        total_kv = dkv[group, rows(4 + core)] + mate_in[group, rows(2)].astype(F32) + near_in[group].astype(F32)
        part = slice(group * D_HEAD, (group + 1) * D_HEAD)
        dk_ref[:, part] = total_kv[:, 0:D_HEAD].astype(BF16)
        dv_ref[:, part] = total_kv[:, D_HEAD : 2 * D_HEAD].astype(BF16)

    for group in range(groups):
        kv_halos[group].wait_near()
        kv_halos[group].wait_far()
        attend(group)
        if group == 0:
            gb_halo.relay()
            x_halo.relay()
            arrived(c_part(4 + core, way), ("c", "far"))
            c_spread(4 + core, "far")
            c_gather(2 + core, "near")
        else:
            send_far(group - 1)

    def decay_through(ths, slot):
        row = ths[rows(slot, 8)]
        return jnp.concatenate([row[i : i + 1] for i in range(8)], axis=1)

    def adjoint_of(ref, k):
        return dot(bc[rows(core + k)], ref[rows(core + k)], (0, 0))

    def ahead(k, factor):
        value = state if factor is None else state * factor[:, 0:half]
        return dot(ga[rows(core + k)], value.astype(BF16), (1, 1))

    def finish_input(part, adjoint):
        last[0:tok] = last[0:tok] + dot(xs[:, part], adjoint, (1, 1))
        dx = dx_acc[:, part] + dot(b_ref[...], adjoint, (1, 0)) * to_end[:, part]
        dx_ref[:, part] = (dx + skip[:, part] * g_ref[:, part].astype(F32)).astype(BF16)

    def sum_start(held, out, into, name, first, last):
        span = pl.ds(first * share, (last - first) * share)
        for j in range(ways):
            for i in range(first, last):
                part = held[i * tok + j * share : i * tok + (j + 1) * share]
                out[j, i * share : (i + 1) * share] = part.astype(BF16)
        for j, peer in enumerate(others):
            put(out.at[peer[1], span], into.at[j, span], peer, (name, first, j))

    def sum_finish(held, into, name, first, last):
        span = pl.ds(first * share, (last - first) * share)
        for j in range(ways - 1):
            arrived(into.at[j, span], (name, first, j))
        values = []
        for i in range(first, last):
            value = held[pl.ds(pl.multiple_of(i * tok + way * share, share), share)]
            for j in range(ways - 1):
                value = value + into[j, i * share : (i + 1) * share].astype(F32)
            values.append(value)
        return values

    def send_ahead(k, value):
        ahead_out[k - 1] = value.astype(BF16)
        put(ahead_out.at[k - 1], ahead_in.at[k - 1], along(k), ("ahead", k))

    first_half, second_half = slice(0, half), slice(half, width)
    ga_halo.wait_near()
    bth_halo.wait_near()
    th1 = decay_through(bth, core + 1)
    early[0:tok] = ahead(1, None)
    early[tok : 2 * tok] = ahead(2, th1)
    sum_start(early, early_out, early_in, "early", 0, 2)
    ga_halo.finish()
    bth_halo.finish()
    send_far(groups - 1)
    bth_halo.wait_far()
    th2 = th1 * decay_through(bth, core + 2)
    th3 = decay_through(bth, core + 3)
    ga_halo.wait_far()
    late[0:tok] = ahead(3, th2)
    late[tok : 2 * tok] = ahead(4, th2 * th3)
    sum_start(late, late_out, late_in, "late", 0, 2)
    x_halo.finish()
    fth_halo.finish()
    gb_halo.finish()
    c_gather(4 + core, "far")
    arrived(bc.at[rows(1 - core)], ("c", "mate", "own"))
    arrived(bc.at[rows(3 - core)], ("c", "mate", "near"))
    near_adjoint[:, first_half] = adjoint_of(ga, 1) + th1[:, first_half] * adjoint_of(ga, 2)
    gb_halo.wait_near()
    near_adjoint[:, second_half] = adjoint_of(gb, 1) + th1[:, second_half] * adjoint_of(gb, 2)
    ahead_1, ahead_2 = sum_finish(early, early_in, "early", 0, 2)
    send_ahead(1, ahead_1)
    send_ahead(2, ahead_2)
    for group in range(groups):
        send_near(group)
    arrived(bc.at[rows(5 - core)], ("c", "mate", "far"))

    def adjoint(ref, part):
        far = adjoint_of(ref, 3) + th3[:, part] * adjoint_of(ref, 4)
        return (near_adjoint[:, part] + th2[:, part] * far).astype(BF16)

    finish_input(first_half, adjoint(ga, first_half))
    ahead_3, ahead_4 = sum_finish(late, late_in, "late", 0, 2)
    send_ahead(3, ahead_3)
    send_ahead(4, ahead_4)

    x_halo.wait_near()
    fth_halo.wait_near()
    fth_halo.wait_far()
    x_halo.wait_far()
    state_in = None
    for k in range(REACH, 0, -1):
        place = 4 + core - k
        value = dot(fx[rows(place), rest:], fx[rows(place), 0:rest], (0, 0))
        state_in = value if state_in is None else value + decay_through(fth, place)[:, half:] * state_in
    last[tok : 2 * tok] = last[tok : 2 * tok] + dot(gb[g_own], state_in.astype(BF16), (1, 1))
    sum_start(last, last_out, last_in, "last", 1, 2)
    gb_halo.wait_far()
    finish_input(second_half, adjoint(gb, second_half))
    sum_start(last, last_out, last_in, "last", 0, 1)
    for group in range(groups):
        finish_keys(group)
    (sum_c,) = sum_finish(last, last_in, "last", 1, 2)
    for k in range(1, REACH + 1):
        arrived(ahead_in.at[k - 1], ("ahead", k))
        sum_c = sum_c + ahead_in[k - 1].astype(F32)
    dc_ref[...] = sum_c.astype(BF16)
    (sum_b,) = sum_finish(last, last_in, "last", 0, 1)
    db_ref[...] = sum_b.astype(BF16)
    for one in started:
        one.wait_send()


def hand_over(*refs):
    count = len(refs) // 2
    for i in range(count):
        refs[count + i][...] = refs[i][...]


def solution(mesh):
    shards, ways = mesh.shape["ctx"], mesh.shape["head"]

    def on_device(queries, keys, values, grad_attn, ssm_input, ssm_b, ssm_c, log_decay, skip_gain, grad_ssm, doc_lengths):
        tok, kw = keys.shape
        width, state = ssm_input.shape[1], ssm_b.shape[1]
        ratio = queries.shape[1] // kw
        groups = kw // D_HEAD
        share = tok // ways
        vmem = pl.BlockSpec(memory_space=pltpu.VMEM)
        hbm = pl.BlockSpec(memory_space=pltpu.HBM)
        held = lambda a: pltpu.VMEM(a.shape, a.dtype)
        skips, lens = skip_gain.reshape(1, -1), doc_lengths.reshape(1, -1)
        shapes = [queries.shape, keys.shape, values.shape, ssm_input.shape, (share, state), (share, state)]
        results = pl.pallas_call(
            lambda *refs: kernel(shards, ways, *refs),
            out_shape=tuple(pltpu.VMEM(shape, BF16) for shape in shapes),
            in_specs=[hbm] * 11,
            out_specs=(vmem,) * 6,
            scratch_shapes=[
                held(queries),
                held(grad_attn),
                held(ssm_input),
                held(ssm_b),
                held(log_decay),
                held(skips),
                held(grad_ssm),
                held(lens),
                pltpu.VMEM((groups, SLOTS * tok, 2 * D_HEAD), BF16),
                pltpu.VMEM((SLOTS * tok, width // 8 * (8 - EIGHTHS) + state), BF16),
                pltpu.VMEM((SLOTS * 8, width // 8), F32),
                pltpu.VMEM((SLOTS * tok, width // 8 * EIGHTHS), BF16),
                pltpu.VMEM((SLOTS * tok, width // 8 * (8 - EIGHTHS)), BF16),
                pltpu.VMEM((SLOTS * tok, state), BF16),
                pltpu.VMEM((SLOTS * 8, width // 8), F32),
                pltpu.VMEM((tok, width), BF16),
                pltpu.VMEM((groups, SLOTS * tok, 2 * D_HEAD), F32),
                pltpu.VMEM((groups, 3 * tok, 2 * D_HEAD), BF16),
                pltpu.VMEM((groups, 3 * tok, 2 * D_HEAD), BF16),
                pltpu.VMEM((groups, tok, 2 * D_HEAD), BF16),
                pltpu.VMEM((groups, tok, 2 * D_HEAD), BF16),
                pltpu.VMEM((groups, tok, 2 * D_HEAD), BF16),
                pltpu.VMEM((groups, tok, 2 * D_HEAD), BF16),
                pltpu.VMEM(((REACH + 1) * tok, ratio * tok), BF16),
                pltpu.VMEM(((REACH + 1) * tok, ratio * tok), BF16),
                pltpu.VMEM((tok, width), F32),
                pltpu.VMEM((tok, width), F32),
                pltpu.VMEM((state, width), F32),
                pltpu.VMEM((2 * tok, state), F32),
                pltpu.VMEM((ways, 2 * share, state), BF16),
                pltpu.VMEM((ways - 1, 2 * share, state), BF16),
                pltpu.VMEM((2 * tok, state), F32),
                pltpu.VMEM((ways, 2 * share, state), BF16),
                pltpu.VMEM((ways - 1, 2 * share, state), BF16),
                pltpu.VMEM((2 * tok, state), F32),
                pltpu.VMEM((ways, 2 * share, state), BF16),
                pltpu.VMEM((ways - 1, 2 * share, state), BF16),
                pltpu.VMEM((REACH, share, state), BF16),
                pltpu.VMEM((REACH, share, state), BF16),
                pltpu.SemaphoreType.DMA((TRANSFERS,)),
                pltpu.SemaphoreType.DMA((TRANSFERS,)),
                pltpu.SemaphoreType.DMA((9 + 2 * groups,)),
                pltpu.SemaphoreType.REGULAR,
            ],
            compiler_params=pltpu.CompilerParams(
                collective_id=0, has_side_effects=True, vmem_limit_bytes=VMEM_BYTES
            ),
        )(
            queries,
            keys,
            values,
            grad_attn,
            ssm_input,
            ssm_b,
            ssm_c,
            log_decay,
            skips,
            grad_ssm,
            lens,
        )
        return pl.pallas_call(
            hand_over,
            out_shape=tuple(jax.ShapeDtypeStruct(shape, BF16) for shape in shapes),
            in_specs=[vmem] * 6,
            out_specs=(vmem,) * 6,
            compiler_params=pltpu.CompilerParams(vmem_limit_bytes=4 * 1024 * 1024),
        )(*results)

    both = P("ctx", "head")
    rows = P(("ctx", "head"), None)
    return jax.shard_map(
        on_device,
        mesh=mesh,
        in_specs=(both, both, both, both, both, P("ctx", None), P("ctx", None), P("head", "ctx"), P("head"), both, P()),
        out_specs=(both, both, both, both, rows, rows),
        check_vma=False,
    )
```

```python
import math

import jax
import jax.numpy as jnp
from jax import lax
from jax.experimental import pallas as pl
from jax.experimental.pallas import tpu as pltpu
from jax.sharding import PartitionSpec as P

D_HEAD = 128
MDIM = 64
REACH = 4
SLOTS = REACH + 2
EIGHTHS = 5
TRANSFERS = 72
VMEM_BYTES = 56 * 1024 * 1024

F32 = jnp.float32
BF16 = jnp.bfloat16
MESH = pl.DeviceIdType.MESH
HIGH = lax.Precision.HIGHEST


def dot(a, b, over, precision=None):
    return lax.dot_general(
        a, b, ((over[:1], over[1:]), ((), ())), precision=precision, preferred_element_type=F32
    )


def iota(shape, dim):
    return lax.broadcasted_iota(jnp.int32, shape, dim)


def document_starts(lens, base, tok):
    docs = lens.shape[1]
    row, col = iota((docs, docs), 0), iota((docs, docs), 1)
    lens_row = jnp.broadcast_to(lens.astype(F32), (docs, docs))
    lens_col = jnp.sum(jnp.where(row == col, lens_row, 0.0), axis=1, keepdims=True)
    ends_col = jnp.sum(jnp.where(col <= row, lens_row, 0.0), axis=1, keepdims=True)
    ends_row = jnp.sum(jnp.where(row <= col, lens_col, 0.0), axis=0, keepdims=True)
    at_col = (base + iota((tok, docs), 0)).astype(F32)
    at_row = (base + iota((docs, tok), 1)).astype(F32)
    start_col = jnp.max(jnp.where(at_col >= ends_row, ends_row, 0.0), axis=1, keepdims=True)
    start_row = jnp.max(jnp.where(at_row >= ends_col, ends_col, 0.0), axis=0, keepdims=True)
    return start_col, start_row


def kernel(
    shards,
    ways,
    q_hbm,
    k_hbm,
    v_hbm,
    do_hbm,
    x_hbm,
    b_hbm,
    c_hbm,
    decay_hbm,
    skip_hbm,
    g_hbm,
    lens_hbm,
    dq_ref,
    dk_ref,
    dv_ref,
    dx_ref,
    db_ref,
    dc_ref,
    q_ref,
    do_ref,
    x_ref,
    b_ref,
    decay_ref,
    skip_ref,
    g_ref,
    lens_ref,
    kv,
    fx,
    fth,
    ga,
    gb,
    bc,
    bth,
    xs,
    dkv,
    mate_out,
    mate_in,
    far_out,
    far_in,
    near_out,
    near_in,
    probs,
    dscores,
    to_end,
    dx_acc,
    near_adjoint,
    early,
    early_out,
    early_in,
    late,
    late_out,
    late_in,
    last,
    last_out,
    last_in,
    ahead_out,
    ahead_in,
    send,
    recv,
    load,
    ready,
):
    tok, heads = q_ref.shape[0], decay_ref.shape[0]
    kw = k_hbm.shape[1]
    groups = kw // D_HEAD
    ratio = q_ref.shape[1] // kw
    width = x_ref.shape[1]
    share = tok // ways
    half = width // 8 * EIGHTHS
    rest = width - half
    shard = lax.axis_index("ctx")
    way = lax.axis_index("head")
    core = lax.rem(shard, 2)

    def along(steps):
        return (lax.rem(shard + (steps + shards), shards), way)

    mate = (shard + 1 - 2 * core, way)
    up, down = along(2), along(-2)
    others = [(shard, lax.rem(way + j, ways)) for j in range(1, ways)]
    barrier = pltpu.get_barrier_semaphore()
    for peer in [along(-1), along(-2), mate] + others:
        pl.semaphore_signal(barrier, inc=1, device_id=peer, device_id_type=MESH)

    def rows(slot, size=tok):
        return pl.ds(pl.multiple_of(slot * size, size), size)

    numbers = {}

    def copy(source, target, peer, name):
        number = numbers.setdefault(name, len(numbers))
        return pltpu.make_async_remote_copy(
            src_ref=source,
            dst_ref=target,
            send_sem=send.at[number],
            recv_sem=recv.at[number],
            device_id=peer,
            device_id_type=MESH,
        )

    started = []

    def put(source, target, peer, name):
        one = copy(source, target, peer, name)
        one.start()
        started.append(one)

    def arrived(target, name):
        copy(target, target, mate, name).wait_recv()

    class Halo:
        def __init__(self, name, upward, view):
            self.name, self.view = name, view
            self.own, self.near, self.far = (4, 2, 0) if upward else (0, 2, 4)
            self.peer = up if upward else down

        def send(self, slot, peer, what, target=None):
            place = self.view(slot if target is None else target)
            put(self.view(slot), place, peer, (self.name, what))

        def begin(self):
            self.send(self.own + core, self.peer, "near", self.near + core)

        def begin_mate(self):
            self.send(self.own + core, mate, "mate own")

        def relay(self):
            arrived(self.view(self.near + core), (self.name, "near"))
            self.send(self.near + core, self.peer, "far", self.far + core)
            self.send(self.near + core, mate, "mate near")

        def finish(self):
            arrived(self.view(self.far + core), (self.name, "far"))
            self.send(self.far + core, mate, "mate far")

        def wait_near(self):
            arrived(self.view(self.own + 1 - core), (self.name, "mate own"))
            arrived(self.view(self.near + 1 - core), (self.name, "mate near"))

        def wait_far(self):
            arrived(self.view(self.far + 1 - core), (self.name, "mate far"))

    kv_halos = [Halo(("kv", i), True, lambda slot, i=i: kv.at[i, rows(slot)]) for i in range(groups)]
    x_halo = Halo("x", True, lambda slot: fx.at[rows(slot)])
    fth_halo = Halo("fth", True, lambda slot: fth.at[rows(slot, 8)])
    ga_halo = Halo("ga", False, lambda slot: ga.at[rows(slot)])
    gb_halo = Halo("gb", False, lambda slot: gb.at[rows(slot)])
    bth_halo = Halo("bth", False, lambda slot: bth.at[rows(slot, 8)])

    def c_part(slot, of):
        return bc.at[pl.ds(pl.multiple_of(slot * tok + of * share, share), share)]

    def c_spread(slot, name):
        for j, peer in enumerate(others):
            put(c_part(slot, way), c_part(slot, way), peer, ("c", name, j))

    def c_gather(slot, name):
        for j in range(ways - 1):
            arrived(c_part(slot, lax.rem(way + (ways - 1 - j), ways)), ("c", name, j))
        put(bc.at[rows(slot)], bc.at[rows(slot)], mate, ("c", "mate", name))

    own = rows(4 + core)
    g_own = rows(core)
    loads = {}
    places = [
        ("lens", lens_hbm, lens_ref),
        ("decay", decay_hbm, decay_ref),
        ("skip", skip_hbm, skip_ref),
    ]
    for i in range(groups):
        part_of = slice(i * D_HEAD, (i + 1) * D_HEAD)
        places.append(("k", k_hbm.at[:, part_of], kv.at[i, own, 0:D_HEAD]))
        places.append(("v", v_hbm.at[:, part_of], kv.at[i, own, D_HEAD : 2 * D_HEAD]))
    places += [
        ("c", c_hbm, bc.at[g_own]),
        ("g", g_hbm, g_ref),
        ("x", x_hbm, x_ref),
        ("b", b_hbm, b_ref),
        ("q", q_hbm, q_ref),
        ("do", do_hbm, do_ref),
    ]
    for number, (name, source, target) in enumerate(places):
        one = pltpu.make_async_copy(source, target, load.at[number])
        one.start()
        loads.setdefault(name, []).append(one)

    def loaded(*names):
        for name in names:
            for one in loads[name]:
                one.wait()

    def pieces(value):
        high = value.astype(BF16)
        middle = (value - high.astype(F32)).astype(BF16)
        return high, middle, (value - high.astype(F32) - middle.astype(F32)).astype(BF16)

    def widen(value, count):
        return sum(dot(piece, spread, (1, 0)) for piece in pieces(value)[:count])

    pl.semaphore_wait(barrier, 3 + len(others))
    pl.semaphore_signal(ready, inc=1, device_id=up, device_id_type=MESH)
    loaded("k", "v")
    for halo in kv_halos:
        halo.begin()
    for halo in kv_halos:
        halo.begin_mate()
    loaded("lens", "decay", "skip")
    base = shard * tok
    base_f = base.astype(F32)
    start_col, start_row = document_starts(lens_ref[...], base, tok)
    later = (iota((tok, tok), 0) >= iota((tok, tok), 1)).astype(BF16)
    decay_pieces = pieces(decay_ref[...])
    cum_col = sum(dot(later, piece, (1, 1)) for piece in decay_pieces)
    carried = jnp.exp(cum_col) * (start_col < base_f).astype(F32)
    spread = (iota((heads, width), 1) // MDIM == iota((heads, width), 0)).astype(BF16)
    total = cum_col[tok - 1 : tok, :]
    last_start = start_col[tok - 1 : tok, :]
    through = jnp.exp(total) * (last_start < base_f).astype(F32)
    table = jnp.concatenate([jnp.broadcast_to(through, (8, heads)), jnp.broadcast_to(skip_ref[...], (8, heads))], axis=0)
    wide = widen(table, 3)
    skip = wide[8:9]
    th = jnp.concatenate([wide[0:1, i * (width // 8) : (i + 1) * (width // 8)] for i in range(8)], axis=0)
    bth[rows(core, 8)] = th
    fth[rows(4 + core, 8)] = th
    fth_halo.begin()
    wide = widen(carried, 2)
    loaded("g", "c")
    ga[g_own] = (g_ref[:, 0:half].astype(F32) * wide[:, 0:half]).astype(BF16)
    gb[g_own] = (g_ref[:, half:].astype(F32) * wide[:, half:]).astype(BF16)
    pl.semaphore_wait(ready, 1)
    put(c_part(core, way), c_part(2 + core, way), down, ("c", "near"))
    bth_halo.begin()
    ga_halo.begin()
    gb_halo.begin()
    to_end[...] = widen(jnp.exp(total - cum_col) * (start_col == last_start).astype(F32), 2)
    loaded("x", "b")
    xs[...] = (x_ref[...].astype(F32) * to_end[...]).astype(BF16)
    fx[own, 0:rest] = xs[:, half:]
    fx[own, rest:] = b_ref[...]
    for halo in (fth_halo, bth_halo, ga_halo, gb_halo, x_halo):
        halo.begin_mate()
    put(bc.at[g_own], bc.at[g_own], mate, ("c", "mate", "own"))
    cum_row = sum(dot(piece, later, (1, 1)) for piece in decay_pieces)
    state = dot(b_ref[...], xs[:, 0:half], (0, 0))

    causal = (iota((tok, tok), 0) >= iota((tok, tok), 1)) & (
        start_col <= (base + iota((tok, tok), 1)).astype(F32)
    )
    couple = dot(bc[g_own], b_ref[...], (1, 1))
    low = iota((tok, 2 * MDIM), 1) < MDIM

    def pair_of_heads(pair, mix):
        part = slice(pair * 2 * MDIM, (pair + 1) * 2 * MDIM)
        grad = g_ref[:, part]
        none = jnp.zeros_like(grad)
        both = jnp.concatenate([jnp.where(low, grad, none), jnp.where(low, none, grad)], axis=0)
        pairs = dot(both, x_ref[:, part], (1, 1))
        within = [
            jnp.exp(jnp.where(causal, cum_col[:, h : h + 1] - cum_row[h : h + 1, :], -1e30))
            for h in (2 * pair, 2 * pair + 1)
        ]
        back = jnp.concatenate([w * couple for w in within], axis=0).astype(BF16)
        dx_acc[:, part] = dot(back, both, (0, 0))
        return mix + pairs[0:tok] * within[0] + pairs[tok : 2 * tok] * within[1]

    mix = jnp.zeros((tok, tok), F32)
    for pair in range(heads // 4):
        mix = pair_of_heads(pair, mix)
    kv_halos[0].relay()
    for pair in range(heads // 4, heads // 2 - 2):
        mix = pair_of_heads(pair, mix)
    for halo in kv_halos[1:]:
        halo.relay()
    x_halo.begin()
    for pair in range(heads // 2 - 2, heads // 2):
        mix = pair_of_heads(pair, mix)
    mix = mix.astype(BF16)
    last[0:tok] = dot(mix, bc[g_own], (0, 0))
    last[tok : 2 * tok] = dot(mix, b_ref[...], (1, 0))
    arrived(c_part(2 + core, way), ("c", "near"))
    put(c_part(2 + core, way), c_part(4 + core, way), down, ("c", "far"))
    c_spread(2 + core, "near")
    bth_halo.relay()
    fth_halo.relay()
    kv_halos[0].finish()
    ga_halo.relay()
    kv_halos[1].finish()

    loaded("q", "do")
    window = (REACH + 1) * tok
    seen = pl.ds(pl.multiple_of(core * tok, tok), window)
    key_at = (base - REACH * tok + iota((window, tok), 0)).astype(F32)
    query_at = (base + iota((window, tok), 1)).astype(F32)
    allowed = (key_at <= query_at) & (key_at >= start_row)
    bias = jnp.where(allowed, 0.0, -1e30)
    bias = jnp.concatenate([bias, bias], axis=1)
    scale = 1.0 / math.sqrt(D_HEAD)
    idle = rows(5 * (1 - core))

    def attend(group):
        keys = kv[group, seen, 0:D_HEAD]
        values = kv[group, seen, D_HEAD : 2 * D_HEAD]
        heads_of = [slice((group * ratio + r) * D_HEAD, (group * ratio + r + 1) * D_HEAD) for r in range(ratio)]
        queries = jnp.concatenate([q_ref[:, part] for part in heads_of], axis=0)
        outgrad = jnp.concatenate([do_ref[:, part] for part in heads_of], axis=0)
        for half in range(ratio // 2):
            part = slice(half * 2 * tok, (half + 1) * 2 * tok)
            scores = dot(keys, queries[part], (1, 1)) * scale + bias
            weights = jnp.exp(scores - jnp.max(scores, axis=0, keepdims=True))
            normed = weights * (1.0 / jnp.sum(weights, axis=0, keepdims=True))
            dprobs = dot(values, outgrad[part], (1, 1))
            centre = jnp.sum(normed * dprobs, axis=0, keepdims=True)
            probs[:, part] = normed.astype(BF16)
            dscores[:, part] = (normed * (dprobs - centre)).astype(BF16)
        dkv[group, idle] = jnp.zeros((tok, 2 * D_HEAD), F32)
        dkv[group, seen, 0:D_HEAD] = dot(dscores[...], queries, (1, 0)) * scale
        dkv[group, seen, D_HEAD : 2 * D_HEAD] = dot(probs[...], outgrad, (1, 0))
        for i in range(3):
            mate_out[group, rows(i)] = dkv[group, rows(2 * i + 1 - core)].astype(BF16)
        put(mate_out.at[group], mate_in.at[group], mate, ("dkv mate", group))
        grad_query = dot(dscores[...], keys, (0, 0)) * scale
        for r, part in enumerate(heads_of):
            dq_ref[:, part] = grad_query[r * tok : (r + 1) * tok].astype(BF16)

    def send_far(group):
        arrived(mate_in.at[group], ("dkv mate", group))
        far_out[group] = (dkv[group, rows(core)] + mate_in[group, rows(0)].astype(F32)).astype(BF16)
        put(far_out.at[group], far_in.at[group], down, ("dkv far", group))

    def send_near(group):
        arrived(far_in.at[group], ("dkv far", group))
        near = dkv[group, rows(2 + core)] + mate_in[group, rows(1)].astype(F32) + far_in[group].astype(F32)
        near_out[group] = near.astype(BF16)
        put(near_out.at[group], near_in.at[group], down, ("dkv near", group))

    def finish_keys(group):
        arrived(near_in.at[group], ("dkv near", group))
        total_kv = dkv[group, rows(4 + core)] + mate_in[group, rows(2)].astype(F32) + near_in[group].astype(F32)
        part = slice(group * D_HEAD, (group + 1) * D_HEAD)
        dk_ref[:, part] = total_kv[:, 0:D_HEAD].astype(BF16)
        dv_ref[:, part] = total_kv[:, D_HEAD : 2 * D_HEAD].astype(BF16)

    for group in range(groups):
        kv_halos[group].wait_near()
        kv_halos[group].wait_far()
        attend(group)
        if group == 0:
            gb_halo.relay()
            x_halo.relay()
            arrived(c_part(4 + core, way), ("c", "far"))
            c_spread(4 + core, "far")
            c_gather(2 + core, "near")
        else:
            send_far(group - 1)

    def decay_through(ths, slot):
        row = ths[rows(slot, 8)]
        return jnp.concatenate([row[i : i + 1] for i in range(8)], axis=1)

    def adjoint_of(ref, k):
        return dot(bc[rows(core + k)], ref[rows(core + k)], (0, 0))

    def ahead(k, factor):
        value = state if factor is None else state * factor[:, 0:half]
        return dot(ga[rows(core + k)], value.astype(BF16), (1, 1))

    def finish_input(part, adjoint):
        last[0:tok] = last[0:tok] + dot(xs[:, part], adjoint, (1, 1))
        dx = dx_acc[:, part] + dot(b_ref[...], adjoint, (1, 0)) * to_end[:, part]
        dx_ref[:, part] = (dx + skip[:, part] * g_ref[:, part].astype(F32)).astype(BF16)

    def sum_start(held, out, into, name, first, last):
        span = pl.ds(first * share, (last - first) * share)
        for j in range(ways):
            for i in range(first, last):
                part = held[i * tok + j * share : i * tok + (j + 1) * share]
                out[j, i * share : (i + 1) * share] = part.astype(BF16)
        for j, peer in enumerate(others):
            put(out.at[peer[1], span], into.at[j, span], peer, (name, first, j))

    def sum_finish(held, into, name, first, last):
        span = pl.ds(first * share, (last - first) * share)
        for j in range(ways - 1):
            arrived(into.at[j, span], (name, first, j))
        values = []
        for i in range(first, last):
            value = held[pl.ds(pl.multiple_of(i * tok + way * share, share), share)]
            for j in range(ways - 1):
                value = value + into[j, i * share : (i + 1) * share].astype(F32)
            values.append(value)
        return values

    def send_ahead(k, value):
        ahead_out[k - 1] = value.astype(BF16)
        put(ahead_out.at[k - 1], ahead_in.at[k - 1], along(k), ("ahead", k))

    first_half, second_half = slice(0, half), slice(half, width)
    ga_halo.wait_near()
    bth_halo.wait_near()
    th1 = decay_through(bth, core + 1)
    early[0:tok] = ahead(1, None)
    early[tok : 2 * tok] = ahead(2, th1)
    sum_start(early, early_out, early_in, "early", 0, 2)
    ga_halo.finish()
    bth_halo.finish()
    send_far(groups - 1)
    bth_halo.wait_far()
    th2 = th1 * decay_through(bth, core + 2)
    th3 = decay_through(bth, core + 3)
    ga_halo.wait_far()
    late[0:tok] = ahead(3, th2)
    late[tok : 2 * tok] = ahead(4, th2 * th3)
    sum_start(late, late_out, late_in, "late", 0, 2)
    x_halo.finish()
    fth_halo.finish()
    gb_halo.finish()
    c_gather(4 + core, "far")
    arrived(bc.at[rows(1 - core)], ("c", "mate", "own"))
    arrived(bc.at[rows(3 - core)], ("c", "mate", "near"))
    near_adjoint[:, first_half] = adjoint_of(ga, 1) + th1[:, first_half] * adjoint_of(ga, 2)
    gb_halo.wait_near()
    near_adjoint[:, second_half] = adjoint_of(gb, 1) + th1[:, second_half] * adjoint_of(gb, 2)
    ahead_1, ahead_2 = sum_finish(early, early_in, "early", 0, 2)
    send_ahead(1, ahead_1)
    send_ahead(2, ahead_2)
    ahead_3, ahead_4 = sum_finish(late, late_in, "late", 0, 2)
    send_ahead(3, ahead_3)
    send_ahead(4, ahead_4)
    for group in range(groups):
        send_near(group)
    arrived(bc.at[rows(5 - core)], ("c", "mate", "far"))

    def adjoint(ref, part):
        far = adjoint_of(ref, 3) + th3[:, part] * adjoint_of(ref, 4)
        return (near_adjoint[:, part] + th2[:, part] * far).astype(BF16)

    finish_input(first_half, adjoint(ga, first_half))

    x_halo.wait_near()
    fth_halo.wait_near()
    fth_halo.wait_far()
    x_halo.wait_far()
    state_in = None
    for k in range(REACH, 0, -1):
        place = 4 + core - k
        value = dot(fx[rows(place), rest:], fx[rows(place), 0:rest], (0, 0))
        state_in = value if state_in is None else value + decay_through(fth, place)[:, half:] * state_in
    last[tok : 2 * tok] = last[tok : 2 * tok] + dot(gb[g_own], state_in.astype(BF16), (1, 1))
    sum_start(last, last_out, last_in, "last", 1, 2)
    gb_halo.wait_far()
    finish_input(second_half, adjoint(gb, second_half))
    sum_start(last, last_out, last_in, "last", 0, 1)
    for group in range(groups):
        finish_keys(group)
    (sum_c,) = sum_finish(last, last_in, "last", 1, 2)
    for k in range(1, REACH + 1):
        arrived(ahead_in.at[k - 1], ("ahead", k))
        sum_c = sum_c + ahead_in[k - 1].astype(F32)
    dc_ref[...] = sum_c.astype(BF16)
    (sum_b,) = sum_finish(last, last_in, "last", 0, 1)
    db_ref[...] = sum_b.astype(BF16)
    for one in started:
        one.wait_send()


def hand_over(*refs):
    count = len(refs) // 2
    for i in range(count):
        refs[count + i][...] = refs[i][...]


def solution(mesh):
    shards, ways = mesh.shape["ctx"], mesh.shape["head"]

    def on_device(queries, keys, values, grad_attn, ssm_input, ssm_b, ssm_c, log_decay, skip_gain, grad_ssm, doc_lengths):
        tok, kw = keys.shape
        width, state = ssm_input.shape[1], ssm_b.shape[1]
        ratio = queries.shape[1] // kw
        groups = kw // D_HEAD
        share = tok // ways
        vmem = pl.BlockSpec(memory_space=pltpu.VMEM)
        hbm = pl.BlockSpec(memory_space=pltpu.HBM)
        held = lambda a: pltpu.VMEM(a.shape, a.dtype)
        skips, lens = skip_gain.reshape(1, -1), doc_lengths.reshape(1, -1)
        shapes = [queries.shape, keys.shape, values.shape, ssm_input.shape, (share, state), (share, state)]
        results = pl.pallas_call(
            lambda *refs: kernel(shards, ways, *refs),
            out_shape=tuple(pltpu.VMEM(shape, BF16) for shape in shapes),
            in_specs=[hbm] * 11,
            out_specs=(vmem,) * 6,
            scratch_shapes=[
                held(queries),
                held(grad_attn),
                held(ssm_input),
                held(ssm_b),
                held(log_decay),
                held(skips),
                held(grad_ssm),
                held(lens),
                pltpu.VMEM((groups, SLOTS * tok, 2 * D_HEAD), BF16),
                pltpu.VMEM((SLOTS * tok, width // 8 * (8 - EIGHTHS) + state), BF16),
                pltpu.VMEM((SLOTS * 8, width // 8), F32),
                pltpu.VMEM((SLOTS * tok, width // 8 * EIGHTHS), BF16),
                pltpu.VMEM((SLOTS * tok, width // 8 * (8 - EIGHTHS)), BF16),
                pltpu.VMEM((SLOTS * tok, state), BF16),
                pltpu.VMEM((SLOTS * 8, width // 8), F32),
                pltpu.VMEM((tok, width), BF16),
                pltpu.VMEM((groups, SLOTS * tok, 2 * D_HEAD), F32),
                pltpu.VMEM((groups, 3 * tok, 2 * D_HEAD), BF16),
                pltpu.VMEM((groups, 3 * tok, 2 * D_HEAD), BF16),
                pltpu.VMEM((groups, tok, 2 * D_HEAD), BF16),
                pltpu.VMEM((groups, tok, 2 * D_HEAD), BF16),
                pltpu.VMEM((groups, tok, 2 * D_HEAD), BF16),
                pltpu.VMEM((groups, tok, 2 * D_HEAD), BF16),
                pltpu.VMEM(((REACH + 1) * tok, ratio * tok), BF16),
                pltpu.VMEM(((REACH + 1) * tok, ratio * tok), BF16),
                pltpu.VMEM((tok, width), F32),
                pltpu.VMEM((tok, width), F32),
                pltpu.VMEM((state, width), F32),
                pltpu.VMEM((2 * tok, state), F32),
                pltpu.VMEM((ways, 2 * share, state), BF16),
                pltpu.VMEM((ways - 1, 2 * share, state), BF16),
                pltpu.VMEM((2 * tok, state), F32),
                pltpu.VMEM((ways, 2 * share, state), BF16),
                pltpu.VMEM((ways - 1, 2 * share, state), BF16),
                pltpu.VMEM((2 * tok, state), F32),
                pltpu.VMEM((ways, 2 * share, state), BF16),
                pltpu.VMEM((ways - 1, 2 * share, state), BF16),
                pltpu.VMEM((REACH, share, state), BF16),
                pltpu.VMEM((REACH, share, state), BF16),
                pltpu.SemaphoreType.DMA((TRANSFERS,)),
                pltpu.SemaphoreType.DMA((TRANSFERS,)),
                pltpu.SemaphoreType.DMA((9 + 2 * groups,)),
                pltpu.SemaphoreType.REGULAR,
            ],
            compiler_params=pltpu.CompilerParams(
                collective_id=0, has_side_effects=True, vmem_limit_bytes=VMEM_BYTES
            ),
        )(
            queries,
            keys,
            values,
            grad_attn,
            ssm_input,
            ssm_b,
            ssm_c,
            log_decay,
            skips,
            grad_ssm,
            lens,
        )
        return pl.pallas_call(
            hand_over,
            out_shape=tuple(jax.ShapeDtypeStruct(shape, BF16) for shape in shapes),
            in_specs=[vmem] * 6,
            out_specs=(vmem,) * 6,
            compiler_params=pltpu.CompilerParams(vmem_limit_bytes=4 * 1024 * 1024),
        )(*results)

    both = P("ctx", "head")
    rows = P(("ctx", "head"), None)
    return jax.shard_map(
        on_device,
        mesh=mesh,
        in_specs=(both, both, both, both, both, P("ctx", None), P("ctx", None), P("head", "ctx"), P("head"), both, P()),
        out_specs=(both, both, both, both, rows, rows),
        check_vma=False,
    )
```

```python
import math

import jax
import jax.numpy as jnp
from jax import lax
from jax.experimental import pallas as pl
from jax.experimental.pallas import tpu as pltpu
from jax.sharding import PartitionSpec as P

D_HEAD = 128
MDIM = 64
REACH = 4
SLOTS = REACH + 2
EIGHTHS = 5
TRANSFERS = 72
VMEM_BYTES = 56 * 1024 * 1024

F32 = jnp.float32
BF16 = jnp.bfloat16
MESH = pl.DeviceIdType.MESH
HIGH = lax.Precision.HIGHEST


def dot(a, b, over, precision=None):
    return lax.dot_general(
        a, b, ((over[:1], over[1:]), ((), ())), precision=precision, preferred_element_type=F32
    )


def iota(shape, dim):
    return lax.broadcasted_iota(jnp.int32, shape, dim)


def document_starts(lens, base, tok):
    docs = lens.shape[1]
    row, col = iota((docs, docs), 0), iota((docs, docs), 1)
    lens_row = jnp.broadcast_to(lens.astype(F32), (docs, docs))
    lens_col = jnp.sum(jnp.where(row == col, lens_row, 0.0), axis=1, keepdims=True)
    ends_col = jnp.sum(jnp.where(col <= row, lens_row, 0.0), axis=1, keepdims=True)
    ends_row = jnp.sum(jnp.where(row <= col, lens_col, 0.0), axis=0, keepdims=True)
    at_col = (base + iota((tok, docs), 0)).astype(F32)
    at_row = (base + iota((docs, tok), 1)).astype(F32)
    start_col = jnp.max(jnp.where(at_col >= ends_row, ends_row, 0.0), axis=1, keepdims=True)
    start_row = jnp.max(jnp.where(at_row >= ends_col, ends_col, 0.0), axis=0, keepdims=True)
    return start_col, start_row


def kernel(
    shards,
    ways,
    q_hbm,
    k_hbm,
    v_hbm,
    do_hbm,
    x_hbm,
    b_hbm,
    c_hbm,
    decay_hbm,
    skip_hbm,
    g_hbm,
    lens_hbm,
    dq_ref,
    dk_ref,
    dv_ref,
    dx_ref,
    db_ref,
    dc_ref,
    q_ref,
    do_ref,
    x_ref,
    b_ref,
    decay_ref,
    skip_ref,
    g_ref,
    lens_ref,
    kv,
    fx,
    fth,
    ga,
    gb,
    bc,
    bth,
    xs,
    dkv,
    mate_out,
    mate_in,
    far_out,
    far_in,
    near_out,
    near_in,
    probs,
    dscores,
    to_end,
    dx_acc,
    near_adjoint,
    early,
    early_out,
    early_in,
    late,
    late_out,
    late_in,
    last,
    last_out,
    last_in,
    ahead_out,
    ahead_in,
    send,
    recv,
    load,
    ready,
):
    tok, heads = q_ref.shape[0], decay_ref.shape[0]
    kw = k_hbm.shape[1]
    groups = kw // D_HEAD
    ratio = q_ref.shape[1] // kw
    width = x_ref.shape[1]
    share = tok // ways
    half = width // 8 * EIGHTHS
    rest = width - half
    shard = lax.axis_index("ctx")
    way = lax.axis_index("head")
    core = lax.rem(shard, 2)

    def along(steps):
        return (lax.rem(shard + (steps + shards), shards), way)

    mate = (shard + 1 - 2 * core, way)
    up, down = along(2), along(-2)
    others = [(shard, lax.rem(way + j, ways)) for j in range(1, ways)]
    barrier = pltpu.get_barrier_semaphore()
    for peer in [along(-1), along(-2), mate] + others:
        pl.semaphore_signal(barrier, inc=1, device_id=peer, device_id_type=MESH)

    def rows(slot, size=tok):
        return pl.ds(pl.multiple_of(slot * size, size), size)

    numbers = {}

    def copy(source, target, peer, name):
        number = numbers.setdefault(name, len(numbers))
        return pltpu.make_async_remote_copy(
            src_ref=source,
            dst_ref=target,
            send_sem=send.at[number],
            recv_sem=recv.at[number],
            device_id=peer,
            device_id_type=MESH,
        )

    started = []

    def put(source, target, peer, name):
        one = copy(source, target, peer, name)
        one.start()
        started.append(one)

    def arrived(target, name):
        copy(target, target, mate, name).wait_recv()

    class Halo:
        def __init__(self, name, upward, view):
            self.name, self.view = name, view
            self.own, self.near, self.far = (4, 2, 0) if upward else (0, 2, 4)
            self.peer = up if upward else down

        def send(self, slot, peer, what, target=None):
            place = self.view(slot if target is None else target)
            put(self.view(slot), place, peer, (self.name, what))

        def begin(self):
            self.send(self.own + core, self.peer, "near", self.near + core)

        def begin_mate(self):
            self.send(self.own + core, mate, "mate own")

        def relay(self):
            arrived(self.view(self.near + core), (self.name, "near"))
            self.send(self.near + core, self.peer, "far", self.far + core)
            self.send(self.near + core, mate, "mate near")

        def finish(self):
            arrived(self.view(self.far + core), (self.name, "far"))
            self.send(self.far + core, mate, "mate far")

        def wait_near(self):
            arrived(self.view(self.own + 1 - core), (self.name, "mate own"))
            arrived(self.view(self.near + 1 - core), (self.name, "mate near"))

        def wait_far(self):
            arrived(self.view(self.far + 1 - core), (self.name, "mate far"))

    kv_halos = [Halo(("kv", i), True, lambda slot, i=i: kv.at[i, rows(slot)]) for i in range(groups)]
    x_halo = Halo("x", True, lambda slot: fx.at[rows(slot)])
    fth_halo = Halo("fth", True, lambda slot: fth.at[rows(slot, 8)])
    ga_halo = Halo("ga", False, lambda slot: ga.at[rows(slot)])
    gb_halo = Halo("gb", False, lambda slot: gb.at[rows(slot)])
    bth_halo = Halo("bth", False, lambda slot: bth.at[rows(slot, 8)])

    def c_part(slot, of):
        return bc.at[pl.ds(pl.multiple_of(slot * tok + of * share, share), share)]

    def c_spread(slot, name):
        for j, peer in enumerate(others):
            put(c_part(slot, way), c_part(slot, way), peer, ("c", name, j))

    def c_gather(slot, name):
        for j in range(ways - 1):
            arrived(c_part(slot, lax.rem(way + (ways - 1 - j), ways)), ("c", name, j))
        put(bc.at[rows(slot)], bc.at[rows(slot)], mate, ("c", "mate", name))

    own = rows(4 + core)
    g_own = rows(core)
    loads = {}
    places = [
        ("lens", lens_hbm, lens_ref),
        ("decay", decay_hbm, decay_ref),
        ("skip", skip_hbm, skip_ref),
    ]
    for i in range(groups):
        part_of = slice(i * D_HEAD, (i + 1) * D_HEAD)
        places.append(("k", k_hbm.at[:, part_of], kv.at[i, own, 0:D_HEAD]))
        places.append(("v", v_hbm.at[:, part_of], kv.at[i, own, D_HEAD : 2 * D_HEAD]))
    places += [
        ("c", c_hbm, bc.at[g_own]),
        ("g", g_hbm, g_ref),
        ("x", x_hbm, x_ref),
        ("b", b_hbm, b_ref),
        ("q", q_hbm, q_ref),
        ("do", do_hbm, do_ref),
    ]
    for number, (name, source, target) in enumerate(places):
        one = pltpu.make_async_copy(source, target, load.at[number])
        one.start()
        loads.setdefault(name, []).append(one)

    def loaded(*names):
        for name in names:
            for one in loads[name]:
                one.wait()

    def pieces(value):
        high = value.astype(BF16)
        middle = (value - high.astype(F32)).astype(BF16)
        return high, middle, (value - high.astype(F32) - middle.astype(F32)).astype(BF16)

    def widen(value, count):
        return sum(dot(piece, spread, (1, 0)) for piece in pieces(value)[:count])

    pl.semaphore_wait(barrier, 3 + len(others))
    pl.semaphore_signal(ready, inc=1, device_id=up, device_id_type=MESH)
    loaded("k", "v")
    for halo in kv_halos:
        halo.begin()
    for halo in kv_halos:
        halo.begin_mate()
    loaded("lens", "decay", "skip")
    base = shard * tok
    base_f = base.astype(F32)
    start_col, start_row = document_starts(lens_ref[...], base, tok)
    later = (iota((tok, tok), 0) >= iota((tok, tok), 1)).astype(BF16)
    decay_pieces = pieces(decay_ref[...])
    cum_col = sum(dot(later, piece, (1, 1)) for piece in decay_pieces)
    carried = jnp.exp(cum_col) * (start_col < base_f).astype(F32)
    spread = (iota((heads, width), 1) // MDIM == iota((heads, width), 0)).astype(BF16)
    total = cum_col[tok - 1 : tok, :]
    last_start = start_col[tok - 1 : tok, :]
    through = jnp.exp(total) * (last_start < base_f).astype(F32)
    table = jnp.concatenate([jnp.broadcast_to(through, (8, heads)), jnp.broadcast_to(skip_ref[...], (8, heads))], axis=0)
    wide = widen(table, 3)
    skip = wide[8:9]
    th = jnp.concatenate([wide[0:1, i * (width // 8) : (i + 1) * (width // 8)] for i in range(8)], axis=0)
    bth[rows(core, 8)] = th
    fth[rows(4 + core, 8)] = th
    fth_halo.begin()
    wide = widen(carried, 2)
    loaded("g", "c")
    ga[g_own] = (g_ref[:, 0:half].astype(F32) * wide[:, 0:half]).astype(BF16)
    gb[g_own] = (g_ref[:, half:].astype(F32) * wide[:, half:]).astype(BF16)
    pl.semaphore_wait(ready, 1)
    put(c_part(core, way), c_part(2 + core, way), down, ("c", "near"))
    bth_halo.begin()
    ga_halo.begin()
    gb_halo.begin()
    to_end[...] = widen(jnp.exp(total - cum_col) * (start_col == last_start).astype(F32), 2)
    loaded("x", "b")
    xs[...] = (x_ref[...].astype(F32) * to_end[...]).astype(BF16)
    fx[own, 0:rest] = xs[:, half:]
    fx[own, rest:] = b_ref[...]
    for halo in (fth_halo, bth_halo, ga_halo, gb_halo, x_halo):
        halo.begin_mate()
    put(bc.at[g_own], bc.at[g_own], mate, ("c", "mate", "own"))
    cum_row = sum(dot(piece, later, (1, 1)) for piece in decay_pieces)
    state = dot(b_ref[...], xs[:, 0:half], (0, 0))

    causal = (iota((tok, tok), 0) >= iota((tok, tok), 1)) & (
        start_col <= (base + iota((tok, tok), 1)).astype(F32)
    )
    couple = dot(bc[g_own], b_ref[...], (1, 1))
    low = iota((tok, 2 * MDIM), 1) < MDIM

    def pair_of_heads(pair, mix):
        part = slice(pair * 2 * MDIM, (pair + 1) * 2 * MDIM)
        grad = g_ref[:, part]
        none = jnp.zeros_like(grad)
        both = jnp.concatenate([jnp.where(low, grad, none), jnp.where(low, none, grad)], axis=0)
        pairs = dot(both, x_ref[:, part], (1, 1))
        within = [
            jnp.exp(jnp.where(causal, cum_col[:, h : h + 1] - cum_row[h : h + 1, :], -1e30))
            for h in (2 * pair, 2 * pair + 1)
        ]
        back = jnp.concatenate([w * couple for w in within], axis=0).astype(BF16)
        dx_acc[:, part] = dot(back, both, (0, 0))
        return mix + pairs[0:tok] * within[0] + pairs[tok : 2 * tok] * within[1]

    mix = jnp.zeros((tok, tok), F32)
    for pair in range(heads // 4):
        mix = pair_of_heads(pair, mix)
    kv_halos[0].relay()
    for pair in range(heads // 4, heads // 2 - 2):
        mix = pair_of_heads(pair, mix)
    for halo in kv_halos[1:]:
        halo.relay()
    x_halo.begin()
    for pair in range(heads // 2 - 2, heads // 2):
        mix = pair_of_heads(pair, mix)
    mix = mix.astype(BF16)
    last[0:tok] = dot(mix, bc[g_own], (0, 0))
    last[tok : 2 * tok] = dot(mix, b_ref[...], (1, 0))
    arrived(c_part(2 + core, way), ("c", "near"))
    put(c_part(2 + core, way), c_part(4 + core, way), down, ("c", "far"))
    c_spread(2 + core, "near")
    bth_halo.relay()
    fth_halo.relay()
    kv_halos[0].finish()
    ga_halo.relay()
    kv_halos[1].finish()

    loaded("q", "do")
    window = (REACH + 1) * tok
    seen = pl.ds(pl.multiple_of(core * tok, tok), window)
    key_at = (base - REACH * tok + iota((window, tok), 0)).astype(F32)
    query_at = (base + iota((window, tok), 1)).astype(F32)
    allowed = (key_at <= query_at) & (key_at >= start_row)
    bias = jnp.where(allowed, 0.0, -1e30)
    bias = jnp.concatenate([bias, bias], axis=1)
    scale = 1.0 / math.sqrt(D_HEAD)
    idle = rows(5 * (1 - core))

    def attend(group):
        keys = kv[group, seen, 0:D_HEAD]
        values = kv[group, seen, D_HEAD : 2 * D_HEAD]
        heads_of = [slice((group * ratio + r) * D_HEAD, (group * ratio + r + 1) * D_HEAD) for r in range(ratio)]
        queries = jnp.concatenate([q_ref[:, part] for part in heads_of], axis=0)
        outgrad = jnp.concatenate([do_ref[:, part] for part in heads_of], axis=0)
        for half in range(ratio // 2):
            part = slice(half * 2 * tok, (half + 1) * 2 * tok)
            scores = dot(keys, queries[part], (1, 1)) * scale + bias
            weights = jnp.exp(scores - jnp.max(scores, axis=0, keepdims=True))
            normed = weights * (1.0 / jnp.sum(weights, axis=0, keepdims=True))
            dprobs = dot(values, outgrad[part], (1, 1))
            centre = jnp.sum(normed * dprobs, axis=0, keepdims=True)
            probs[:, part] = normed.astype(BF16)
            dscores[:, part] = (normed * (dprobs - centre)).astype(BF16)
        dkv[group, idle] = jnp.zeros((tok, 2 * D_HEAD), F32)
        dkv[group, seen, 0:D_HEAD] = dot(dscores[...], queries, (1, 0)) * scale
        dkv[group, seen, D_HEAD : 2 * D_HEAD] = dot(probs[...], outgrad, (1, 0))
        for i in range(3):
            mate_out[group, rows(i)] = dkv[group, rows(2 * i + 1 - core)].astype(BF16)
        put(mate_out.at[group], mate_in.at[group], mate, ("dkv mate", group))
        grad_query = dot(dscores[...], keys, (0, 0)) * scale
        for r, part in enumerate(heads_of):
            dq_ref[:, part] = grad_query[r * tok : (r + 1) * tok].astype(BF16)

    def send_far(group):
        arrived(mate_in.at[group], ("dkv mate", group))
        far_out[group] = (dkv[group, rows(core)] + mate_in[group, rows(0)].astype(F32)).astype(BF16)
        put(far_out.at[group], far_in.at[group], down, ("dkv far", group))

    def send_near(group):
        arrived(far_in.at[group], ("dkv far", group))
        near = dkv[group, rows(2 + core)] + mate_in[group, rows(1)].astype(F32) + far_in[group].astype(F32)
        near_out[group] = near.astype(BF16)
        put(near_out.at[group], near_in.at[group], down, ("dkv near", group))

    def finish_keys(group):
        arrived(near_in.at[group], ("dkv near", group))
        total_kv = dkv[group, rows(4 + core)] + mate_in[group, rows(2)].astype(F32) + near_in[group].astype(F32)
        part = slice(group * D_HEAD, (group + 1) * D_HEAD)
        dk_ref[:, part] = total_kv[:, 0:D_HEAD].astype(BF16)
        dv_ref[:, part] = total_kv[:, D_HEAD : 2 * D_HEAD].astype(BF16)

    for group in range(groups):
        kv_halos[group].wait_near()
        kv_halos[group].wait_far()
        attend(group)
        if group == 0:
            gb_halo.relay()
            x_halo.relay()
            arrived(c_part(4 + core, way), ("c", "far"))
            c_spread(4 + core, "far")
            c_gather(2 + core, "near")
        else:
            send_far(group - 1)

    def decay_through(ths, slot):
        row = ths[rows(slot, 8)]
        return jnp.concatenate([row[i : i + 1] for i in range(8)], axis=1)

    def adjoint_of(ref, k):
        return dot(bc[rows(core + k)], ref[rows(core + k)], (0, 0))

    def ahead(k, factor):
        value = state if factor is None else state * factor[:, 0:half]
        return dot(ga[rows(core + k)], value.astype(BF16), (1, 1))

    def finish_input(part, adjoint):
        last[0:tok] = last[0:tok] + dot(xs[:, part], adjoint, (1, 1))
        dx = dx_acc[:, part] + dot(b_ref[...], adjoint, (1, 0)) * to_end[:, part]
        dx_ref[:, part] = (dx + skip[:, part] * g_ref[:, part].astype(F32)).astype(BF16)

    def sum_start(held, out, into, name, first, last):
        span = pl.ds(first * share, (last - first) * share)
        for j in range(ways):
            for i in range(first, last):
                part = held[i * tok + j * share : i * tok + (j + 1) * share]
                out[j, i * share : (i + 1) * share] = part.astype(BF16)
        for j, peer in enumerate(others):
            put(out.at[peer[1], span], into.at[j, span], peer, (name, first, j))

    def sum_finish(held, into, name, first, last):
        span = pl.ds(first * share, (last - first) * share)
        for j in range(ways - 1):
            arrived(into.at[j, span], (name, first, j))
        values = []
        for i in range(first, last):
            value = held[pl.ds(pl.multiple_of(i * tok + way * share, share), share)]
            for j in range(ways - 1):
                value = value + into[j, i * share : (i + 1) * share].astype(F32)
            values.append(value)
        return values

    def send_ahead(k, value):
        ahead_out[k - 1] = value.astype(BF16)
        put(ahead_out.at[k - 1], ahead_in.at[k - 1], along(k), ("ahead", k))

    first_half, second_half = slice(0, half), slice(half, width)
    ga_halo.wait_near()
    bth_halo.wait_near()
    th1 = decay_through(bth, core + 1)
    early[0:tok] = ahead(1, None)
    early[tok : 2 * tok] = ahead(2, th1)
    sum_start(early, early_out, early_in, "early", 0, 2)
    ga_halo.finish()
    bth_halo.finish()
    send_far(groups - 1)
    bth_halo.wait_far()
    th2 = th1 * decay_through(bth, core + 2)
    th3 = decay_through(bth, core + 3)
    ga_halo.wait_far()
    late[0:tok] = ahead(3, th2)
    late[tok : 2 * tok] = ahead(4, th2 * th3)
    sum_start(late, late_out, late_in, "late", 0, 2)
    x_halo.finish()
    fth_halo.finish()
    gb_halo.finish()
    c_gather(4 + core, "far")
    arrived(bc.at[rows(1 - core)], ("c", "mate", "own"))
    arrived(bc.at[rows(3 - core)], ("c", "mate", "near"))
    near_adjoint[:, first_half] = adjoint_of(ga, 1) + th1[:, first_half] * adjoint_of(ga, 2)
    gb_halo.wait_near()
    near_adjoint[:, second_half] = adjoint_of(gb, 1) + th1[:, second_half] * adjoint_of(gb, 2)
    ahead_1, ahead_2 = sum_finish(early, early_in, "early", 0, 2)
    send_ahead(1, ahead_1)
    send_ahead(2, ahead_2)
    ahead_3, ahead_4 = sum_finish(late, late_in, "late", 0, 2)
    send_ahead(3, ahead_3)
    send_ahead(4, ahead_4)
    for group in range(groups):
        send_near(group)
    arrived(bc.at[rows(5 - core)], ("c", "mate", "far"))

    def adjoint(ref, part):
        far = adjoint_of(ref, 3) + th3[:, part] * adjoint_of(ref, 4)
        return (near_adjoint[:, part] + th2[:, part] * far).astype(BF16)

    finish_input(first_half, adjoint(ga, first_half))

    x_halo.wait_near()
    fth_halo.wait_near()
    fth_halo.wait_far()
    x_halo.wait_far()
    state_in = None
    for k in range(REACH, 0, -1):
        place = 4 + core - k
        value = dot(fx[rows(place), rest:], fx[rows(place), 0:rest], (0, 0))
        state_in = value if state_in is None else value + decay_through(fth, place)[:, half:] * state_in
    last[tok : 2 * tok] = last[tok : 2 * tok] + dot(gb[g_own], state_in.astype(BF16), (1, 1))
    sum_start(last, last_out, last_in, "last", 1, 2)
    gb_halo.wait_far()
    finish_input(second_half, adjoint(gb, second_half))
    sum_start(last, last_out, last_in, "last", 0, 1)
    recent = 16
    for one in started[:-recent]:
        one.wait_send()
    for group in range(groups):
        finish_keys(group)
    (sum_c,) = sum_finish(last, last_in, "last", 1, 2)
    for k in range(1, REACH + 1):
        arrived(ahead_in.at[k - 1], ("ahead", k))
        sum_c = sum_c + ahead_in[k - 1].astype(F32)
    dc_ref[...] = sum_c.astype(BF16)
    (sum_b,) = sum_finish(last, last_in, "last", 0, 1)
    db_ref[...] = sum_b.astype(BF16)
    for one in started[-recent:]:
        one.wait_send()


def hand_over(*refs):
    count = len(refs) // 2
    for i in range(count):
        refs[count + i][...] = refs[i][...]


def solution(mesh):
    shards, ways = mesh.shape["ctx"], mesh.shape["head"]

    def on_device(queries, keys, values, grad_attn, ssm_input, ssm_b, ssm_c, log_decay, skip_gain, grad_ssm, doc_lengths):
        tok, kw = keys.shape
        width, state = ssm_input.shape[1], ssm_b.shape[1]
        ratio = queries.shape[1] // kw
        groups = kw // D_HEAD
        share = tok // ways
        vmem = pl.BlockSpec(memory_space=pltpu.VMEM)
        hbm = pl.BlockSpec(memory_space=pltpu.HBM)
        held = lambda a: pltpu.VMEM(a.shape, a.dtype)
        skips, lens = skip_gain.reshape(1, -1), doc_lengths.reshape(1, -1)
        shapes = [queries.shape, keys.shape, values.shape, ssm_input.shape, (share, state), (share, state)]
        results = pl.pallas_call(
            lambda *refs: kernel(shards, ways, *refs),
            out_shape=tuple(pltpu.VMEM(shape, BF16) for shape in shapes),
            in_specs=[hbm] * 11,
            out_specs=(vmem,) * 6,
            scratch_shapes=[
                held(queries),
                held(grad_attn),
                held(ssm_input),
                held(ssm_b),
                held(log_decay),
                held(skips),
                held(grad_ssm),
                held(lens),
                pltpu.VMEM((groups, SLOTS * tok, 2 * D_HEAD), BF16),
                pltpu.VMEM((SLOTS * tok, width // 8 * (8 - EIGHTHS) + state), BF16),
                pltpu.VMEM((SLOTS * 8, width // 8), F32),
                pltpu.VMEM((SLOTS * tok, width // 8 * EIGHTHS), BF16),
                pltpu.VMEM((SLOTS * tok, width // 8 * (8 - EIGHTHS)), BF16),
                pltpu.VMEM((SLOTS * tok, state), BF16),
                pltpu.VMEM((SLOTS * 8, width // 8), F32),
                pltpu.VMEM((tok, width), BF16),
                pltpu.VMEM((groups, SLOTS * tok, 2 * D_HEAD), F32),
                pltpu.VMEM((groups, 3 * tok, 2 * D_HEAD), BF16),
                pltpu.VMEM((groups, 3 * tok, 2 * D_HEAD), BF16),
                pltpu.VMEM((groups, tok, 2 * D_HEAD), BF16),
                pltpu.VMEM((groups, tok, 2 * D_HEAD), BF16),
                pltpu.VMEM((groups, tok, 2 * D_HEAD), BF16),
                pltpu.VMEM((groups, tok, 2 * D_HEAD), BF16),
                pltpu.VMEM(((REACH + 1) * tok, ratio * tok), BF16),
                pltpu.VMEM(((REACH + 1) * tok, ratio * tok), BF16),
                pltpu.VMEM((tok, width), F32),
                pltpu.VMEM((tok, width), F32),
                pltpu.VMEM((state, width), F32),
                pltpu.VMEM((2 * tok, state), F32),
                pltpu.VMEM((ways, 2 * share, state), BF16),
                pltpu.VMEM((ways - 1, 2 * share, state), BF16),
                pltpu.VMEM((2 * tok, state), F32),
                pltpu.VMEM((ways, 2 * share, state), BF16),
                pltpu.VMEM((ways - 1, 2 * share, state), BF16),
                pltpu.VMEM((2 * tok, state), F32),
                pltpu.VMEM((ways, 2 * share, state), BF16),
                pltpu.VMEM((ways - 1, 2 * share, state), BF16),
                pltpu.VMEM((REACH, share, state), BF16),
                pltpu.VMEM((REACH, share, state), BF16),
                pltpu.SemaphoreType.DMA((TRANSFERS,)),
                pltpu.SemaphoreType.DMA((TRANSFERS,)),
                pltpu.SemaphoreType.DMA((9 + 2 * groups,)),
                pltpu.SemaphoreType.REGULAR,
            ],
            compiler_params=pltpu.CompilerParams(
                collective_id=0, has_side_effects=True, vmem_limit_bytes=VMEM_BYTES
            ),
        )(
            queries,
            keys,
            values,
            grad_attn,
            ssm_input,
            ssm_b,
            ssm_c,
            log_decay,
            skips,
            grad_ssm,
            lens,
        )
        return pl.pallas_call(
            hand_over,
            out_shape=tuple(jax.ShapeDtypeStruct(shape, BF16) for shape in shapes),
            in_specs=[vmem] * 6,
            out_specs=(vmem,) * 6,
            compiler_params=pltpu.CompilerParams(vmem_limit_bytes=4 * 1024 * 1024),
        )(*results)

    both = P("ctx", "head")
    rows = P(("ctx", "head"), None)
    return jax.shard_map(
        on_device,
        mesh=mesh,
        in_specs=(both, both, both, both, both, P("ctx", None), P("ctx", None), P("head", "ctx"), P("head"), both, P()),
        out_specs=(both, both, both, both, rows, rows),
        check_vma=False,
    )
```
